256 devices in a mesh: lat: 4 (over y_hi, core), lon: 64 (over z, y_lo, x).
Axes of the slice: x: 4, y: 4 (y_hi: 2, y_lo: 2; y = y_hi * 2 + y_lo), z: 8, core: 2. Of those that a mesh axis runs over, the one named last changes fastest.
Arguments:
- grid_latent: bfloat16 [4, 64, 128, 512], P('lat', 'lon'), may hold values from -16 to 16
- grid_cot: bfloat16 [4, 64, 128, 512], P('lat', 'lon'), may hold values from -6 to 6
- mesh_latent: bfloat16 [4, 64, 64, 512], P('lat', 'lon'), may hold values from -16 to 16
- mesh_cot: bfloat16 [4, 64, 64, 512], P('lat', 'lon'), may hold values from -6 to 6
- processed: bfloat16 [4, 64, 64, 512], P('lat', 'lon'), may hold values from -16 to 16
- enc_weights: bfloat16 [3, 512, 512], replicated, may hold values from -0.25 to 0.25
- dec_weights: bfloat16 [3, 512, 512], replicated, may hold values from -0.25 to 0.25
- enc_send: int32 [4, 64, 2, 128], P('lat', 'lon'), may hold values from 0 to 127
- enc_recv: int32 [4, 64, 2, 128], P('lat', 'lon'), may hold values from 0 to 575, as said below
- enc_live: int32 [4, 64, 1], P('lat', 'lon'), may hold values from 64 to 256
- dec_send: int32 [4, 64, 3, 128], P('lat', 'lon'), may hold values from 0 to 575, as said below
- dec_recv: int32 [4, 64, 3, 128], P('lat', 'lon'), may hold values from 0 to 127
Outputs:
- grid_grad: bfloat16 [4, 64, 128, 512], P('lat', 'lon')
- mesh_grad: bfloat16 [4, 64, 64, 512], P('lat', 'lon')
- proc_grad: bfloat16 [4, 64, 64, 512], P('lat', 'lon')
- enc_grads: float32 [3, 512, 512], P(None, 'lon')
- dec_grads: float32 [3, 512, 512], P(None, 'lon')
The draws below stay inside these ranges and needn't reach their ends.
Inputs may be any that keep to these rules, and one draw needn't show every extreme that they name: `enc_recv`: row e names slot e // 64 = 3 a + b of the extended block (band offset a - 1, sector offset b - 1, sectors closed in a cycle); no edge names a band outside the grid. `dec_send`: row e names slot e // 64 = 3 a + b of the extended block (band offset a - 1, sector offset b - 1, sectors closed in a cycle); no edge names a band outside the grid. The first enc_live[t] slots of tile t are live.
All inputs are finite; a program needn't handle non-finite values.
Results may differ from the reference program's by a relative error of at most 0.006.
Values may be sent and summed in bfloat16 or wider, within the bound.
A program may use at most 128 MiB of HBM per device.

```python
import math
import jax
import jax.numpy as jnp
from jax import lax

D = 512
TILE = 128
TILES_DEV = 1
MESH_DEV = 64
ENC_PER_TILE = 2
DEC_PER_TILE = 3
BANDS = 4
SECTORS = 64
GRID_DEV = 128
ENC_BLOCKS = 2
DEC_BLOCKS = 3


def mesh_rows_drawn(seed_key, blocks):
    key_slot, key_row = jax.random.split(seed_key)
    grid_shape = (BANDS, SECTORS, blocks, TILE)
    pick_draw = jax.random.randint(key_slot, grid_shape, 0, 16)
    other_slot = jnp.clip(pick_draw - 8, 0, 7)
    other_slot = other_slot + (other_slot >= 4).astype(jnp.int32)
    slot_index = jnp.where(pick_draw < 8, 4, other_slot)
    band_index = lax.broadcasted_iota(jnp.int32, grid_shape, 0)
    slot_index = jnp.where((band_index == 0) & (slot_index < 3), slot_index + 3, slot_index)
    slot_index = jnp.where((band_index == BANDS - 1) & (slot_index >= 6), slot_index - 3, slot_index)
    local_row = jax.random.randint(key_row, grid_shape, 0, MESH_DEV)
    return (slot_index * MESH_DEV + local_row).astype(jnp.int32)


def draw_enc_recv(key, part):
    key = jax.random.fold_in(key, 11)
    return mesh_rows_drawn(key, ENC_BLOCKS)


def draw_dec_send(key, part):
    key = jax.random.fold_in(key, 12)
    return mesh_rows_drawn(key, DEC_BLOCKS)


def plant(array, own_key, least, high):
    spot = [jax.random.randint(jax.random.fold_in(own_key, axis), (), 0, length) for axis, length in enumerate(array.shape)]
    widest = array.shape.index(max(array.shape))
    beside = spot[:widest] + [(spot[widest] + 1) % array.shape[widest]] + spot[widest + 1:]
    return array.at[tuple(spot)].set(least).at[tuple(beside)].set(high)


def raised(result, rng, source, target, shards_of, factor):
    owner, partner = [(jnp.arange(result.shape[axis_at]) // (result.shape[axis_at] // shards_of)).reshape([-1 if axis == axis_at else 1 for axis in range(result.ndim)]) for axis_at in (source, target)]
    chosen = jax.random.permutation(rng, shards_of)[partner]
    strong = (owner == chosen) | (owner == (partner + shards_of // 2) % shards_of)
    return jnp.where(strong, factor * result, result)


def level_of(rng, extent, cuts, smallest, top_value):
    def one(position, parts):
        steps = jax.random.uniform(jax.random.fold_in(jax.random.fold_in(rng, 6), position), (parts,), jnp.float32, smallest / len(cuts), top_value / len(cuts))
        return jnp.repeat(jnp.exp(steps), extent[position] // parts).reshape((-1,) + (1,) * (len(extent) - position - 1))

    loudness = one(*cuts[0])
    for cut in cuts[1:]:
        loudness = loudness * one(*cut)
    return loudness


def gaussian(stream_key, shape, scale, limit, shards=(), held_as=jnp.bfloat16):
    values = scale * jax.random.normal(stream_key, shape, jnp.float32)
    if shards:
        values = values * level_of(stream_key, shape, shards, -0.22, 0.18)
    return jnp.clip(values, -limit, limit).astype(held_as)


def heavy_noise(rng, extent, spread, most, cuts, heavy, held_as=jnp.bfloat16):
    drawn = spread * jax.random.normal(rng, extent, jnp.float32)
    if cuts:
        drawn = drawn * level_of(rng, extent, cuts, -0.22, 0.18)
    return jnp.clip(raised(drawn, jax.random.fold_in(rng, 3), *heavy), -most, most).astype(held_as)


def setup_inputs(seed: int = 0) -> dict:
    streams_of = jax.random.split(jax.random.key(seed), 13)
    grid_latent = heavy_noise(streams_of[0], (BANDS, SECTORS, GRID_DEV, D), 1.0, 16.0, ((0, 4), (1, 64)), (1, 3, 64, 4.0))
    grid_cot = gaussian(streams_of[1], (BANDS, SECTORS, GRID_DEV, D), 1.0, 6.0, ((0, 4), (1, 64)))
    mesh_latent = heavy_noise(streams_of[2], (BANDS, SECTORS, MESH_DEV, D), 1.0, 16.0, ((0, 4), (1, 64)), (1, 3, 64, 4.0))
    mesh_cot = gaussian(streams_of[3], (BANDS, SECTORS, MESH_DEV, D), 1.0, 6.0, ((0, 4), (1, 64)))
    processed = heavy_noise(streams_of[4], (BANDS, SECTORS, MESH_DEV, D), 1.0, 16.0, ((0, 4), (1, 64)), (1, 3, 64, 4.0))
    enc_weights = gaussian(streams_of[5], (3, D, D), D ** -0.5, 0.25)
    dec_weights = gaussian(streams_of[6], (3, D, D), D ** -0.5, 0.25)
    enc_send = plant(jax.random.randint(streams_of[7], (BANDS, SECTORS, ENC_BLOCKS, TILE), 0, TILE), jax.random.fold_in(streams_of[7], 1), 0, TILE - 1).astype(jnp.int32)
    enc_recv = draw_enc_recv(jax.random.fold_in(streams_of[12], 71), 0)
    enc_live = plant(jax.random.randint(streams_of[9], (BANDS, SECTORS, TILES_DEV), ENC_PER_TILE * TILE // 4, ENC_PER_TILE * TILE + 1), jax.random.fold_in(streams_of[9], 1), ENC_PER_TILE * TILE // 4, ENC_PER_TILE * TILE).astype(jnp.int32)
    dec_send = draw_dec_send(jax.random.fold_in(streams_of[12], 71), 0)
    dec_recv = plant(jax.random.randint(streams_of[11], (BANDS, SECTORS, DEC_BLOCKS, TILE), 0, TILE), jax.random.fold_in(streams_of[11], 1), 0, TILE - 1).astype(jnp.int32)
    return {"grid_latent": grid_latent, "grid_cot": grid_cot, "mesh_latent": mesh_latent, "mesh_cot": mesh_cot, "processed": processed, "enc_weights": enc_weights, "dec_weights": dec_weights, "enc_send": enc_send, "enc_recv": enc_recv, "enc_live": enc_live, "dec_send": dec_send, "dec_recv": dec_recv}


def silu_slope(values):
    gate_sig = jax.nn.sigmoid(values)
    return gate_sig * (1.0 + values * (1.0 - gate_sig))

def pick_block(stack, band_index, sector_index):
    return lax.dynamic_index_in_dim(lax.dynamic_index_in_dim(stack, band_index, 0, False), sector_index, 0, False)

def pad_bands(stack):
    return jnp.pad(stack, ((1, 1), (0, 0), (0, 0), (0, 0)))

def extend(padded, band_index, sector_index):
    pieces = []
    for row_slot in range(3):
        for col_slot in range(3):
            column = (sector_index + (col_slot - 1 + SECTORS)) % SECTORS
            pieces.append(pick_block(padded, band_index + row_slot, column))
    return jnp.concatenate(pieces, 0)

def scatter_slots(accum, part_rows, band_index, sector_index):
    blocks = part_rows.reshape(9, MESH_DEV, part_rows.shape[1])
    zero_index = jnp.zeros((), jnp.int32)
    for row_slot in range(3):
        for col_slot in range(3):
            column = (sector_index + (col_slot - 1 + SECTORS)) % SECTORS
            current = pick_block(accum, band_index + row_slot, column)
            updated = current + blocks[row_slot * 3 + col_slot]
            accum = lax.dynamic_update_slice(accum, updated[None, None], (band_index + row_slot, column, zero_index, zero_index))
    return accum

def edge_backward(pre_act, cot_picked, live_mask, out_weight):
    hidden = jax.nn.silu(pre_act).astype(jnp.bfloat16)
    msg_grad = jnp.where(live_mask[:, None], cot_picked, jnp.zeros_like(cot_picked))
    pre_grad = (jnp.dot(msg_grad, out_weight.T, preferred_element_type=jnp.float32) * silu_slope(pre_act)).astype(jnp.bfloat16)
    out_grad = jnp.dot(hidden.T, msg_grad, preferred_element_type=jnp.float32)
    return (pre_grad, out_grad)

def reference(grid_latent, grid_cot, mesh_latent, mesh_cot, processed, enc_weights, dec_weights, enc_send, enc_recv, enc_live, dec_send, dec_recv):
    enc_grid_w = enc_weights[0]
    enc_mesh_w = enc_weights[1]
    enc_out_w = enc_weights[2]
    dec_mesh_w = dec_weights[0]
    dec_grid_w = dec_weights[1]
    dec_out_w = dec_weights[2]
    mesh_enc = pad_bands(jnp.dot(mesh_latent, enc_mesh_w, preferred_element_type=jnp.float32).astype(jnp.bfloat16))
    proc_dec = pad_bands(jnp.dot(processed, dec_mesh_w, preferred_element_type=jnp.float32).astype(jnp.bfloat16))
    cot_pad = pad_bands(mesh_cot)
    ext_rows = 9 * MESH_DEV
    enc_edge = jnp.arange(ENC_BLOCKS * TILE, dtype=jnp.int32)
    enc_tile = enc_edge // (ENC_PER_TILE * TILE)
    enc_place = enc_edge % (ENC_PER_TILE * TILE)
    dec_edge = jnp.arange(DEC_BLOCKS * TILE, dtype=jnp.int32)
    dec_tile = dec_edge // (DEC_PER_TILE * TILE)
    dec_mask = dec_edge >= 0

    def per_device(state_in, flat_index):
        weight_sum, mesh_acc, proc_acc = state_in
        band_index = flat_index // SECTORS
        sector_index = flat_index % SECTORS
        grid_rows = pick_block(grid_latent, band_index, sector_index)
        cot_rows = pick_block(grid_cot, band_index, sector_index)
        grid_enc = jnp.dot(grid_rows, enc_grid_w, preferred_element_type=jnp.float32).astype(jnp.bfloat16)
        grid_dec = jnp.dot(grid_rows, dec_grid_w, preferred_element_type=jnp.float32).astype(jnp.bfloat16)
        mesh_ext = extend(mesh_enc, band_index, sector_index)
        cot_ext = extend(cot_pad, band_index, sector_index)
        proc_ext = extend(proc_dec, band_index, sector_index)
        senders = enc_tile * TILE + pick_block(enc_send, band_index, sector_index).reshape(-1)
        receivers = pick_block(enc_recv, band_index, sector_index).reshape(-1)
        enc_mask = enc_place < pick_block(enc_live, band_index, sector_index)[enc_tile]
        enc_pre = grid_enc[senders].astype(jnp.float32) + mesh_ext[receivers].astype(jnp.float32)
        enc_pre_grad, enc_out_grad = edge_backward(enc_pre, cot_ext[receivers], enc_mask, enc_out_w)
        enc_grid_sum = jax.ops.segment_sum(enc_pre_grad.astype(jnp.float32), senders, num_segments=GRID_DEV).astype(jnp.bfloat16)
        enc_mesh_part = jax.ops.segment_sum(enc_pre_grad.astype(jnp.float32), receivers, num_segments=ext_rows)
        mesh_senders = pick_block(dec_send, band_index, sector_index).reshape(-1)
        grid_receivers = dec_tile * TILE + pick_block(dec_recv, band_index, sector_index).reshape(-1)
        dec_pre = proc_ext[mesh_senders].astype(jnp.float32) + grid_dec[grid_receivers].astype(jnp.float32)
        dec_pre_grad, dec_out_grad = edge_backward(dec_pre, cot_rows[grid_receivers], dec_mask, dec_out_w)
        dec_grid_sum = jax.ops.segment_sum(dec_pre_grad.astype(jnp.float32), grid_receivers, num_segments=GRID_DEV).astype(jnp.bfloat16)
        dec_mesh_part = jax.ops.segment_sum(dec_pre_grad.astype(jnp.float32), mesh_senders, num_segments=ext_rows)
        grid_grad = (cot_rows.astype(jnp.float32) + jnp.dot(enc_grid_sum, enc_grid_w.T, preferred_element_type=jnp.float32) + jnp.dot(dec_grid_sum, dec_grid_w.T, preferred_element_type=jnp.float32)).astype(jnp.bfloat16)
        weight_sum = weight_sum + jnp.stack([jnp.dot(grid_rows.T, enc_grid_sum, preferred_element_type=jnp.float32), enc_out_grad, jnp.dot(grid_rows.T, dec_grid_sum, preferred_element_type=jnp.float32), dec_out_grad])
        mesh_acc = scatter_slots(mesh_acc, enc_mesh_part, band_index, sector_index)
        proc_acc = scatter_slots(proc_acc, dec_mesh_part, band_index, sector_index)
        return ((weight_sum, mesh_acc, proc_acc), grid_grad)
    start = (jnp.zeros((4, D, D), jnp.float32), jnp.zeros((BANDS + 2, SECTORS, MESH_DEV, D), jnp.float32), jnp.zeros((BANDS + 2, SECTORS, MESH_DEV, D), jnp.float32))
    (weight_sum, mesh_acc, proc_acc), grid_stack = lax.scan(per_device, start, jnp.arange(BANDS * SECTORS, dtype=jnp.int32))
    grid_grad = grid_stack.reshape(BANDS, SECTORS, GRID_DEV, D)
    enc_mesh_sum = mesh_acc[1:-1].astype(jnp.bfloat16)
    dec_mesh_sum = proc_acc[1:-1].astype(jnp.bfloat16)
    mesh_grad = (mesh_cot.astype(jnp.float32) + jnp.dot(enc_mesh_sum, enc_mesh_w.T, preferred_element_type=jnp.float32)).astype(jnp.bfloat16)
    proc_grad = jnp.dot(dec_mesh_sum, dec_mesh_w.T, preferred_element_type=jnp.float32).astype(jnp.bfloat16)
    mesh_weight = jnp.dot(mesh_latent.reshape(-1, D).T, enc_mesh_sum.reshape(-1, D), preferred_element_type=jnp.float32)
    proc_weight = jnp.dot(processed.reshape(-1, D).T, dec_mesh_sum.reshape(-1, D), preferred_element_type=jnp.float32)
    grad_scale = 1.0 / math.sqrt(BANDS * SECTORS * GRID_DEV)
    enc_grads = jnp.stack([weight_sum[0], mesh_weight, weight_sum[1]]) * grad_scale
    dec_grads = jnp.stack([proc_weight, weight_sum[2], weight_sum[3]]) * grad_scale
    return (grid_grad, mesh_grad, proc_grad, enc_grads, dec_grads)
```

```python
import math

import jax
import jax.numpy as jnp
from jax import lax
from jax.experimental import pallas as pl
from jax.experimental.pallas import tpu as pltpu
from jax.sharding import PartitionSpec as P

BF16 = jnp.bfloat16
F32 = jnp.float32
I32 = jnp.int32
MESH = pl.DeviceIdType.MESH
D = 512
GRID = 128
NODES = 64
SLOTS = 9
EXT = SLOTS * NODES


def dot(a, b):
    return lax.dot_general(a, b, (((1,), (0,)), ((), ())), preferred_element_type=F32)


def dot_bt(a, b):
    return lax.dot_general(a, b, (((1,), (1,)), ((), ())), preferred_element_type=F32)


def dot_at(a, b):
    return lax.dot_general(a, b, (((0,), (0,)), ((), ())), preferred_element_type=F32)


def pick_rows(index_row, rows):
    return jnp.where(lax.broadcasted_iota(I32, (rows, 128), 0) == index_row, 1.0, 0.0).astype(BF16)


def pick_cols(index_row, columns):
    turned = jnp.transpose(jnp.broadcast_to(index_row, (128, 128)))
    lane = lax.broadcasted_iota(I32, (128, 128), 1)
    parts = []
    for start in range(0, columns, 128):
        part = jnp.where(turned == lane + start, 1.0, 0.0).astype(BF16)
        parts.append(part[:, : min(128, columns - start)])
    return parts[0] if len(parts) == 1 else jnp.concatenate(parts, 1)


def kernel(
    grid_ref,
    cot_ref,
    mesh_ref,
    mcot_ref,
    proc_ref,
    encw_ref,
    decw_ref,
    index_ref,
    grid_out,
    mesh_out,
    proc_out,
    enc_out,
    dec_out,
    wts,
    gall,
    call,
    mext,
    text,
    town,
    ibuf,
    gproj,
    mproj,
    gpart,
    back,
    hid,
    msg,
    pgrad,
    part,
    gsum,
    gboth,
    fold,
    dwbuf,
    send1,
    recv1,
    send2,
    recv2,
    send3,
    recv3,
    final,
    w_sem,
    own_sem,
    i_sem,
    g_sem,
    c_sem,
    m_sem,
    t_sem,
    f_sem,
    gs_sem,
    r1_sem,
    r2_sem,
    r3_sem,
    r4_sem,
    hs_sem,
    ss_sem,
    fs_sem,
    s1_sem,
    s2_sem,
    s3_sem,
    s4_sem,
    grad_scale,
):
    lat = lax.axis_index("lat")
    lon = lax.axis_index("lon")
    yh = lax.div(lat, 2)
    core = lax.rem(lat, 2)
    z = lax.div(lon, 8)
    yl = lax.rem(lax.div(lon, 4), 2)
    x = lax.rem(lon, 4)
    y = yh * 2 + yl
    sib = (yh * 2 + (1 - core), lon)
    adjacent = core == 1 - yh

    def lon_of(zz, yy, xx):
        return zz * 8 + yy * 4 + xx

    def sector(step):
        return lax.rem(lon + step + 64, 64)

    def x_dev(xx):
        return (lat, lon_of(z, yl, xx))

    def y_dev(yy):
        return (lax.div(yy, 2) * 2 + core, lon_of(z, lax.rem(yy, 2), x))

    def z_dev(zz):
        return (lat, lon_of(zz, yl, x))

    def rcopy(src, dst, ssem, rsem, dev):
        return pltpu.make_async_remote_copy(
            src_ref=src, dst_ref=dst, send_sem=ssem, recv_sem=rsem, device_id=dev, device_id_type=MESH
        )

    def arrived(dst, rsem):
        pltpu.make_async_copy(dst, dst, rsem).wait()

    def load(src, dst, sem):
        pltpu.make_async_copy(src, dst, sem).start()

    load(encw_ref.at[0], wts.at[0], w_sem.at[0])
    load(decw_ref.at[1], wts.at[3], w_sem.at[3])
    load(encw_ref.at[1], wts.at[1], w_sem.at[1])
    load(decw_ref.at[0], wts.at[2], w_sem.at[2])

    @pl.when(core == 0)
    def _():
        load(encw_ref.at[2], wts.at[4], w_sem.at[4])
        load(index_ref.at[pl.ds(0, 8)], ibuf.at[0], i_sem.at[0])
        load(mesh_ref, mext.at[pl.ds(pl.multiple_of((yh * 3 + 1) * NODES, NODES), NODES)], m_sem.at[yh * 3 + 1])
        load(mcot_ref, text.at[pl.ds(pl.multiple_of((yh * 3 + 1) * NODES, NODES), NODES)], t_sem.at[yh * 3 + 1])

    @pl.when(core == 1)
    def _():
        load(decw_ref.at[2], wts.at[4], w_sem.at[4])
        load(index_ref.at[pl.ds(8, 8)], ibuf.at[1], i_sem.at[1])
        slot = (yh + 1) * 3 + 1
        load(proc_ref, mext.at[pl.ds(pl.multiple_of(slot * NODES, NODES), NODES)], m_sem.at[slot])

    own_rows = pl.ds(pl.multiple_of(core * GRID, GRID), GRID)
    load(grid_ref, gall.at[own_rows], g_sem.at[core])
    load(cot_ref, call.at[own_rows], c_sem.at[core])
    load(mcot_ref, town, own_sem)

    barrier = pltpu.get_barrier_semaphore()
    greeted = []
    for dyh in (0, 1):
        for dc in (0, 1):
            for step in (-1, 0, 1):
                if (dyh, dc, step) != (0, 0, 0):
                    to_yh = yh if dyh == 0 else 1 - yh
                    to_core = core if dc == 0 else 1 - core
                    greeted.append((to_yh * 2 + to_core, sector(step)))
    for step in range(1, 4):
        greeted.append(x_dev(lax.rem(x + step, 4)))
        greeted.append(y_dev(lax.rem(y + step, 4)))
    for step in range(1, 8):
        greeted.append(z_dev(lax.rem(z + step, 8)))
    for dev in greeted:
        pl.semaphore_signal(barrier, inc=1, device_id=dev, device_id_type=MESH)
    pl.semaphore_wait(barrier, len(greeted))

    def halo_copies(side, step):
        to_yh = yh if side == 0 else 1 - yh
        slot = (lat - to_yh) * 3 + 1 - step
        rows = pl.ds(pl.multiple_of(slot * NODES, NODES), NODES)
        at = side * 9 + (step + 1) * 3
        enc_dev = (to_yh * 2, sector(step))
        dec_dev = (to_yh * 2 + 1, sector(step))
        return (
            rcopy(mesh_ref, mext.at[rows], hs_sem.at[at], m_sem.at[slot], enc_dev),
            rcopy(mcot_ref, text.at[rows], hs_sem.at[at + 1], t_sem.at[slot], enc_dev),
            rcopy(proc_ref, mext.at[rows], hs_sem.at[at + 2], m_sem.at[slot], dec_dev),
        )

    def each_halo(action):
        @pl.when(adjacent)
        def _():
            for step in (0, 1, -1):
                for copy in halo_copies(1, step):
                    action(copy)

        for step in (1, -1):
            for copy in halo_copies(0, step):
                action(copy)

        to_mesh, to_mcot, to_proc = halo_copies(0, 0)

        @pl.when(core == 0)
        def _():
            action(to_proc)

        @pl.when(core == 1)
        def _():
            action(to_mesh)
            action(to_mcot)

    def each_swap(action):
        action(rcopy(grid_ref, gall.at[own_rows], ss_sem.at[0], g_sem.at[core], sib))

        @pl.when(core == 0)
        def _():
            action(rcopy(index_ref.at[pl.ds(8, 8)], ibuf.at[0], ss_sem.at[1], i_sem.at[0], sib))
            action(rcopy(cot_ref, call.at[pl.ds(0, GRID)], ss_sem.at[2], c_sem.at[0], sib))

        @pl.when(core == 1)
        def _():
            action(rcopy(index_ref.at[pl.ds(0, 8)], ibuf.at[1], ss_sem.at[1], i_sem.at[1], sib))

    each_swap(lambda copy: copy.start())
    each_halo(lambda copy: copy.start())

    @pl.when(jnp.logical_not(adjacent))
    def _():
        for role in (0, 1):
            for k in (3, 4, 5):
                fold[role, k] = jnp.zeros((NODES, D), BF16)

    def stage1_copies(mat, half):
        copies = []
        for step in (1, 3, 2):
            if half == 0:
                to = lax.rem(x + step, 4)
                dev = x_dev(to)
            else:
                to = lax.rem(y + step, 4)
                dev = y_dev(to)
            sem = (mat * 2 + half) * 3 + step - 1
            copies.append(
                rcopy(send1.at[mat, half, to], recv1.at[mat, half, step - 1], s1_sem.at[sem], r1_sem.at[sem], dev)
            )
        return copies

    def stage2_copies(mat, half):
        copies = []
        for step in (1, 3, 2):
            if half == 0:
                to = lax.rem(y + step, 4)
                dev = y_dev(to)
            else:
                to = lax.rem(x + step, 4)
                dev = x_dev(to)
            sem = (mat * 2 + half) * 3 + step - 1
            copies.append(
                rcopy(send2.at[mat, half, to], recv2.at[mat, half, step - 1], s2_sem.at[sem], r2_sem.at[sem], dev)
            )
        return copies

    def send_matrix(mat):
        for xx in range(4):
            pieces = []
            for yy in range(4):
                for zz in range(4):
                    row = ((yy // 2) * 4 + zz) * 64 + (yy % 2) * 32 + xx * 8
                    pieces.append(dwbuf[row : row + 8, 0:256])
            send1[mat, 0, xx] = jnp.concatenate(pieces, 0).astype(BF16)
        for yy in range(4):
            pieces = []
            for xx in range(4):
                for zz in range(4):
                    row = ((yy // 2) * 4 + zz) * 64 + (yy % 2) * 32 + xx * 8
                    pieces.append(dwbuf[row : row + 8, 256:512])
            send1[mat, 1, yy] = jnp.concatenate(pieces, 0).astype(BF16)
        for half in (0, 1):
            for copy in stage1_copies(mat, half):
                copy.start()

    def fold_copies(k_side, step):
        if k_side == 0:
            out = []
            for to_core in (0, 1):
                slot = (yh + to_core) * 3 + 1 + step
                out.append((to_core, slot, (yh * 2 + to_core, sector(step))))
        else:
            slot = (2 - 2 * yh) * 3 + 1 + step
            out = [(2, slot, ((1 - yh) * 2 + yh, sector(step)))]
        copies = []
        for which, slot, dev in out:
            rows = pl.ds(pl.multiple_of(slot * NODES, NODES), NODES)
            k = k_side * 3 + 1 - step
            copies.append(
                rcopy(part.at[rows], fold.at[core, k], fs_sem.at[which * 3 + step + 1], f_sem.at[core * 6 + k], dev)
            )
        return copies

    def each_fold(action):
        for step in (0, 1, -1):
            for copy in fold_copies(1, step):
                action(copy)
        for step in (1, -1):
            for copy in fold_copies(0, step):
                action(copy)
        to_first, to_second = fold_copies(0, 0)

        @pl.when(core == 0)
        def _():
            action(to_second)

        @pl.when(core == 1)
        def _():
            action(to_first)

    def gsum_copy():
        other = pl.ds(pl.multiple_of((1 - core) * GRID, GRID), GRID)
        return rcopy(gsum.at[other], gboth.at[core], ss_sem.at[3], gs_sem, sib)

    def weight(k):
        pltpu.make_async_copy(wts.at[k], wts.at[k], w_sem.at[k]).wait()

    def wait_band(band, with_cot):
        for col in range(3):
            slot = band * 3 + col
            rows = pl.ds(pl.multiple_of(slot * NODES, NODES), NODES)
            arrived(mext.at[rows], m_sem.at[slot])

    def wait_cot(band):
        for col in range(3):
            slot = band * 3 + col
            rows = pl.ds(pl.multiple_of(slot * NODES, NODES), NODES)
            arrived(text.at[rows], t_sem.at[slot])

    def network(role):
        blocks = 2 if role == 0 else 3
        edges = blocks * 128
        w_grid, w_mesh = (0, 1) if role == 0 else (3, 2)
        for band in (0, 1):
            arrived(gall.at[pl.ds(band * GRID, GRID)], g_sem.at[band])
        weight(w_grid)
        gproj[...] = dot(gall[...], wts[w_grid]).astype(BF16)
        for band in (0, 1):
            arrived(ibuf.at[band], i_sem.at[band])
        index = [ibuf[band] for band in (0, 1)]
        grid_rows = [[index[b][(0 if role == 0 else 3) + q : (0 if role == 0 else 3) + q + 1] for q in range(blocks)] for b in (0, 1)]
        shift = [192 * (yh + b - 1) for b in (0, 1)]
        mesh_rows = [
            [index[b][(2 if role == 0 else 0) + q : (2 if role == 0 else 0) + q + 1] + shift[b] for q in range(blocks)]
            for b in (0, 1)
        ]
        weight(4)
        for b in (0, 1):
            rows = slice(b * edges, (b + 1) * edges)
            g_pick = jnp.concatenate([pick_cols(r, GRID) for r in grid_rows[b]], 0)
            gpart[rows] = dot(g_pick, gproj[b * GRID : (b + 1) * GRID])
            if role == 1:
                arrived(call.at[pl.ds(b * GRID, GRID)], c_sem.at[b])
                picked = dot(g_pick, call[b * GRID : (b + 1) * GRID]).astype(BF16)
                msg[rows] = picked
                back[rows] = dot_bt(picked, wts[4])
        weight(w_mesh)
        for k in (0, 1, 2):
            band = (yh + k if k < 2 else 2 - 2 * yh)
            wait_band(band, role == 0)
            rows = pl.ds(pl.multiple_of(band * 192, 192), 192)
            mproj[rows] = dot(mext[rows], wts[w_mesh]).astype(BF16)
        if role == 0:
            for band in range(3):
                wait_cot(band)
        for b in (0, 1):
            rows = slice(b * edges, (b + 1) * edges)
            m_pick = jnp.concatenate([pick_cols(r, EXT) for r in mesh_rows[b]], 0)
            pre = dot(m_pick, mproj[...]) + gpart[rows]
            if role == 0:
                place = lax.broadcasted_iota(I32, (edges, D), 0)
                live = index[b][4:5, 0:1]
                picked = jnp.where(place < live, dot(m_pick, text[...]), 0.0).astype(BF16)
                msg[rows] = picked
                grown = dot_bt(picked, wts[4])
            else:
                grown = back[rows]
            gate = 1.0 / (1.0 + jnp.exp(-pre))
            hid[rows] = (pre * gate).astype(BF16)
            pgrad[rows] = (grown * (gate * (1.0 + pre * (1.0 - gate)))).astype(BF16)
        every = slice(0, 2 * edges)
        dwbuf[...] = dot_at(hid[every], msg[every])
        send_matrix(2)
        m_turn = jnp.concatenate([pick_rows(r, EXT) for b in (0, 1) for r in mesh_rows[b]], 1)
        part[...] = dot(m_turn, pgrad[every]).astype(BF16)
        each_fold(lambda copy: copy.start())
        dwbuf[...] = dot_at(mext[...], part[...])
        send_matrix(1 if role == 0 else 0)
        for b in (0, 1):
            g_turn = jnp.concatenate([pick_rows(r, GRID) for r in grid_rows[b]], 1)
            gsum[b * GRID : (b + 1) * GRID] = dot(g_turn, pgrad[b * edges : (b + 1) * edges]).astype(BF16)
        gsum_copy().start()
        dwbuf[...] = dot_at(gall[...], gsum[...])
        send_matrix(0 if role == 0 else 1)

    @pl.when(core == 0)
    def _():
        network(0)

    @pl.when(core == 1)
    def _():
        network(1)

    @pl.when(core == 0)
    def _():
        for k in (2, 3):
            weight(k)
        arrived(call.at[own_rows], c_sem.at[0])

    @pl.when(core == 1)
    def _():
        for k in (0, 1):
            weight(k)

    arrived(town, own_sem)

    for mat in (2, 0, 1):
        for half in (0, 1):
            for step in range(3):
                sem = (mat * 2 + half) * 3 + step
                arrived(recv1.at[mat, half, step], r1_sem.at[sem])
            own = x if half == 0 else y
            total = send1[mat, half, own].astype(F32)
            for step in range(3):
                total = total + recv1[mat, half, step].astype(F32)
            total = total.astype(BF16)
            for k in range(4):
                send2[mat, half, k] = total[k * 32 : (k + 1) * 32]
            for copy in stage2_copies(mat, half):
                copy.start()

    gboth[core] = gsum[own_rows]
    arrived(gboth.at[1 - core], gs_sem)
    grid_out[...] = (call[own_rows].astype(F32) + dot_bt(gboth[0], wts[0]) + dot_bt(gboth[1], wts[3])).astype(BF16)

    sums = []
    for mat in range(3):
        for half in (0, 1):
            for step in range(3):
                sem = (mat * 2 + half) * 3 + step
                arrived(recv2.at[mat, half, step], r2_sem.at[sem])
            own = y if half == 0 else x
            total = send2[mat, half, own].astype(F32)
            for step in range(3):
                total = total + recv2[mat, half, step].astype(F32)
            sums.append(total)
    for q in range(4):
        send3[q] = jnp.concatenate([s[q * 8 : (q + 1) * 8] for s in sums], 0).astype(BF16)

    holds = lax.div(z, 4) == yh

    def stage3_copy(step):
        to = lax.rem(z + step, 8)
        return (
            lax.div(to, 4) == yh,
            rcopy(send3.at[lax.rem(to, 4)], recv3.at[step - 1], s3_sem.at[step - 1], r3_sem.at[step - 1], z_dev(to)),
        )

    for step in (4, 3, 5, 2, 6, 1, 7):
        goes, copy = stage3_copy(step)
        pl.when(goes)(copy.start)

    def fold_wait(role, k):
        arrived(fold.at[role, k], f_sem.at[role * 6 + k])

    for role in (0, 1):
        for k in (0, 2):
            fold_wait(role, k)
    own_slot = pl.ds(pl.multiple_of(((yh + core) * 3 + 1) * NODES, NODES), NODES)

    @pl.when(core == 0)
    def _():
        fold_wait(1, 1)
        fold[0, 1] = part[own_slot]

    @pl.when(core == 1)
    def _():
        fold_wait(0, 1)
        fold[1, 1] = part[own_slot]

    @pl.when(adjacent)
    def _():
        for role in (0, 1):
            for k in (3, 4, 5):
                fold_wait(role, k)

    def folded(role):
        total = fold[role, 0].astype(F32)
        for k in range(1, 6):
            total = total + fold[role, k].astype(F32)
        return total.astype(BF16)

    mesh_out[...] = (town[...].astype(F32) + dot_bt(folded(0), wts[1])).astype(BF16)
    proc_out[...] = dot_bt(folded(1), wts[2]).astype(BF16)

    def last_copies():
        return (
            rcopy(final.at[core], final.at[core], s4_sem.at[0], r4_sem.at[core], sib),
            rcopy(final.at[core], final.at[core], s4_sem.at[1], r4_sem.at[core], ((1 - yh) * 2 + core, lon)),
            rcopy(final.at[core], final.at[core], s4_sem.at[2], r4_sem.at[core], ((1 - yh) * 2 + 1 - core, lon)),
        )

    @pl.when(holds)
    def _():
        total = send3[lax.rem(z, 4)].astype(F32)
        for step in (1, 7, 2, 6, 3, 5, 4):
            arrived(recv3.at[step - 1], r3_sem.at[step - 1])
            total = total + recv3[step - 1].astype(F32)
        total = total * grad_scale
        pieces = []
        for mat in range(3):
            low = total[mat * 16 : mat * 16 + 8]
            high = total[mat * 16 + 8 : mat * 16 + 16]
            pieces.append(jnp.concatenate([low, high], 1))
        final[core] = jnp.concatenate(pieces, 0)
        for copy in last_copies():
            copy.start()
        arrived(final.at[1 - core], r4_sem.at[1 - core])

    @pl.when(jnp.logical_not(holds))
    def _():
        arrived(final.at[0], r4_sem.at[0])
        arrived(final.at[1], r4_sem.at[1])

    enc_out[...] = final[0]
    dec_out[...] = final[1]

    each_swap(lambda copy: copy.wait_send())
    each_halo(lambda copy: copy.wait_send())
    each_fold(lambda copy: copy.wait_send())
    gsum_copy().wait_send()
    for mat in range(3):
        for half in (0, 1):
            for copy in stage1_copies(mat, half) + stage2_copies(mat, half):
                copy.wait_send()
    for step in range(1, 8):
        goes, copy = stage3_copy(step)
        pl.when(goes)(copy.wait_send)

    @pl.when(holds)
    def _():
        for copy in last_copies():
            copy.wait_send()


def shards(
    grid_latent,
    grid_cot,
    mesh_latent,
    mesh_cot,
    processed,
    enc_weights,
    dec_weights,
    enc_send,
    enc_recv,
    enc_live,
    dec_send,
    dec_recv,
):
    index = jnp.concatenate(
        [
            enc_send[0, 0],
            enc_recv[0, 0],
            jnp.broadcast_to(enc_live[0], (4, 128)),
            dec_send[0, 0],
            dec_recv[0, 0],
            jnp.zeros((2, 128), I32),
        ],
        0,
    )
    grad_scale = 1.0 / math.sqrt(4 * 64 * 128)
    vmem = pltpu.VMEM
    dma = pltpu.SemaphoreType.DMA
    outs = pl.pallas_call(
        lambda *refs: kernel(*refs, grad_scale),
        out_shape=(
            jax.ShapeDtypeStruct((GRID, D), BF16),
            jax.ShapeDtypeStruct((NODES, D), BF16),
            jax.ShapeDtypeStruct((NODES, D), BF16),
            jax.ShapeDtypeStruct((24, D), F32),
            jax.ShapeDtypeStruct((24, D), F32),
        ),
        in_specs=[pl.BlockSpec(memory_space=pl.ANY)] * 8,
        out_specs=(pl.BlockSpec(memory_space=pltpu.VMEM),) * 5,
        scratch_shapes=[
            vmem((5, D, D), BF16),
            vmem((2 * GRID, D), BF16),
            vmem((2 * GRID, D), BF16),
            vmem((EXT, D), BF16),
            vmem((EXT, D), BF16),
            vmem((NODES, D), BF16),
            vmem((2, 8, 128), I32),
            vmem((2 * GRID, D), BF16),
            vmem((EXT, D), BF16),
            vmem((768, D), F32),
            vmem((768, D), F32),
            vmem((768, D), BF16),
            vmem((768, D), BF16),
            vmem((768, D), BF16),
            vmem((EXT, D), BF16),
            vmem((2 * GRID, D), BF16),
            vmem((2, GRID, D), BF16),
            vmem((2, 6, NODES, D), BF16),
            vmem((D, D), F32),
            vmem((3, 2, 4, 128, 256), BF16),
            vmem((3, 2, 3, 128, 256), BF16),
            vmem((3, 2, 4, 32, 256), BF16),
            vmem((3, 2, 3, 32, 256), BF16),
            vmem((4, 48, 256), BF16),
            vmem((7, 48, 256), BF16),
            vmem((2, 24, D), F32),
            dma((5,)),
            dma,
            dma((2,)),
            dma((2,)),
            dma((2,)),
            dma((9,)),
            dma((9,)),
            dma((12,)),
            dma,
            dma((18,)),
            dma((18,)),
            dma((7,)),
            dma((2,)),
            dma((18,)),
            dma((4,)),
            dma((9,)),
            dma((18,)),
            dma((18,)),
            dma((7,)),
            dma((3,)),
        ],
        compiler_params=pltpu.CompilerParams(
            collective_id=0, has_side_effects=True, vmem_limit_bytes=48 * 2**20
        ),
        name="edge_layer",
    )(
        grid_latent[0, 0],
        grid_cot[0, 0],
        mesh_latent[0, 0],
        mesh_cot[0, 0],
        processed[0, 0],
        enc_weights,
        dec_weights,
        index,
    )
    grid_grad, mesh_grad, proc_grad, enc_grads, dec_grads = outs
    return (
        grid_grad[None, None],
        mesh_grad[None, None],
        proc_grad[None, None],
        enc_grads.reshape(3, 8, D),
        dec_grads.reshape(3, 8, D),
    )


def solution(mesh):
    by_node = P("lat", "lon", None, None)
    return jax.shard_map(
        shards,
        mesh=mesh,
        in_specs=(by_node,) * 5 + (P(), P()) + (by_node, by_node, P("lat", "lon", None), by_node, by_node),
        out_specs=(by_node, by_node, by_node, P(None, "lon", None), P(None, "lon", None)),
        check_vma=False,
    )
```

```python
import math

import jax
import jax.numpy as jnp
from jax import lax
from jax.experimental import pallas as pl
from jax.experimental.pallas import tpu as pltpu
from jax.sharding import PartitionSpec as P

BF16 = jnp.bfloat16
F32 = jnp.float32
I32 = jnp.int32
MESH = pl.DeviceIdType.MESH
D = 512
GRID = 128
NODES = 64
SLOTS = 9
EXT = SLOTS * NODES


def dot(a, b):
    return lax.dot_general(a, b, (((1,), (0,)), ((), ())), preferred_element_type=F32)


def dot_bt(a, b):
    return lax.dot_general(a, b, (((1,), (1,)), ((), ())), preferred_element_type=F32)


def dot_at(a, b):
    return lax.dot_general(a, b, (((0,), (0,)), ((), ())), preferred_element_type=F32)


def pick_rows(index_row, rows):
    return jnp.where(lax.broadcasted_iota(I32, (rows, 128), 0) == index_row, 1.0, 0.0).astype(BF16)


def pick_cols(index_row, columns):
    turned = jnp.transpose(jnp.broadcast_to(index_row, (128, 128)))
    lane = lax.broadcasted_iota(I32, (128, 128), 1)
    parts = []
    for start in range(0, columns, 128):
        part = jnp.where(turned == lane + start, 1.0, 0.0).astype(BF16)
        parts.append(part[:, : min(128, columns - start)])
    return parts[0] if len(parts) == 1 else jnp.concatenate(parts, 1)


def kernel(
    grid_ref,
    cot_ref,
    mesh_ref,
    mcot_ref,
    proc_ref,
    encw_ref,
    decw_ref,
    esend_ref,
    erecv_ref,
    live_ref,
    dsend_ref,
    drecv_ref,
    grid_out,
    mesh_out,
    proc_out,
    weights_out,
    wts,
    gall,
    call,
    mext,
    text,
    town,
    ebuf,
    dbuf,
    lbuf,
    lone,
    gproj,
    mproj,
    gpart,
    back,
    hid,
    msg,
    pgrad,
    part,
    gsum,
    gboth,
    fold,
    dwbuf,
    send1,
    recv1,
    send2,
    recv2,
    send3,
    recv3,
    final,
    w_sem,
    own_sem,
    i_sem,
    g_sem,
    c_sem,
    m_sem,
    t_sem,
    f_sem,
    gs_sem,
    r1_sem,
    r2_sem,
    r3_sem,
    r4_sem,
    hs_sem,
    ss_sem,
    fs_sem,
    s1_sem,
    s2_sem,
    s3_sem,
    s4_sem,
    grad_scale,
):
    lat = lax.axis_index("lat")
    lon = lax.axis_index("lon")
    yh = lax.div(lat, 2)
    core = lax.rem(lat, 2)
    z = lax.div(lon, 8)
    yl = lax.rem(lax.div(lon, 4), 2)
    x = lax.rem(lon, 4)
    y = yh * 2 + yl
    sib = (yh * 2 + (1 - core), lon)
    adjacent = core == 1 - yh

    def lon_of(zz, yy, xx):
        return zz * 8 + yy * 4 + xx

    def sector(step):
        return lax.rem(lon + step + 64, 64)

    def x_dev(xx):
        return (lat, lon_of(z, yl, xx))

    def y_dev(yy):
        return (lax.div(yy, 2) * 2 + core, lon_of(z, lax.rem(yy, 2), x))

    def z_dev(zz):
        return (lat, lon_of(zz, yl, x))

    def rcopy(src, dst, ssem, rsem, dev):
        return pltpu.make_async_remote_copy(
            src_ref=src, dst_ref=dst, send_sem=ssem, recv_sem=rsem, device_id=dev, device_id_type=MESH
        )

    def arrived(dst, rsem):
        pltpu.make_async_copy(dst, dst, rsem).wait()

    def load(src, dst, sem):
        pltpu.make_async_copy(src, dst, sem).start()

    load(encw_ref.at[0], wts.at[0], w_sem.at[0])
    load(decw_ref.at[1], wts.at[3], w_sem.at[3])
    load(encw_ref.at[1], wts.at[1], w_sem.at[1])
    load(decw_ref.at[0], wts.at[2], w_sem.at[2])

    @pl.when(core == 0)
    def _():
        load(encw_ref.at[2], wts.at[4], w_sem.at[4])
        load(esend_ref, ebuf.at[0, 0], i_sem.at[0])
        load(erecv_ref, ebuf.at[0, 1], i_sem.at[1])
        load(mesh_ref, mext.at[pl.ds(pl.multiple_of((yh * 3 + 1) * NODES, NODES), NODES)], m_sem.at[yh * 3 + 1])
        load(mcot_ref, text.at[pl.ds(pl.multiple_of((yh * 3 + 1) * NODES, NODES), NODES)], t_sem.at[yh * 3 + 1])

    @pl.when(core == 1)
    def _():
        load(decw_ref.at[2], wts.at[4], w_sem.at[4])
        load(dsend_ref, dbuf.at[1, 0], i_sem.at[2])
        load(drecv_ref, dbuf.at[1, 1], i_sem.at[3])
        slot = (yh + 1) * 3 + 1
        load(proc_ref, mext.at[pl.ds(pl.multiple_of(slot * NODES, NODES), NODES)], m_sem.at[slot])

    own_rows = pl.ds(pl.multiple_of(core * GRID, GRID), GRID)
    load(grid_ref, gall.at[own_rows], g_sem.at[core])
    load(cot_ref, call.at[own_rows], c_sem.at[core])
    load(mcot_ref, town, own_sem.at[0])
    load(live_ref, lone, own_sem.at[1])

    barrier = pltpu.get_barrier_semaphore()
    greeted = []
    for dyh in (0, 1):
        for dc in (0, 1):
            for step in (-1, 0, 1):
                if (dyh, dc, step) != (0, 0, 0):
                    to_yh = yh if dyh == 0 else 1 - yh
                    to_core = core if dc == 0 else 1 - core
                    greeted.append((to_yh * 2 + to_core, sector(step)))
    for step in range(1, 4):
        greeted.append(x_dev(lax.rem(x + step, 4)))
        greeted.append(y_dev(lax.rem(y + step, 4)))
    for step in range(1, 8):
        greeted.append(z_dev(lax.rem(z + step, 8)))
    for dev in greeted:
        pl.semaphore_signal(barrier, inc=1, device_id=dev, device_id_type=MESH)
    pl.semaphore_wait(barrier, len(greeted))

    def halo_copies(side, step):
        to_yh = yh if side == 0 else 1 - yh
        slot = (lat - to_yh) * 3 + 1 - step
        rows = pl.ds(pl.multiple_of(slot * NODES, NODES), NODES)
        at = side * 9 + (step + 1) * 3
        enc_dev = (to_yh * 2, sector(step))
        dec_dev = (to_yh * 2 + 1, sector(step))
        return (
            rcopy(mesh_ref, mext.at[rows], hs_sem.at[at], m_sem.at[slot], enc_dev),
            rcopy(mcot_ref, text.at[rows], hs_sem.at[at + 1], t_sem.at[slot], enc_dev),
            rcopy(proc_ref, mext.at[rows], hs_sem.at[at + 2], m_sem.at[slot], dec_dev),
        )

    def each_halo(which, action):
        @pl.when(adjacent)
        def _():
            for step in (1, -1, 0):
                for w in which:
                    action(halo_copies(1, step)[w])

        for step in (1, -1):
            for w in which:
                action(halo_copies(0, step)[w])

        @pl.when(core == (0 if 2 in which else 1))
        def _():
            for w in which:
                action(halo_copies(0, 0)[w])

    cross_band = 2 - 2 * yh

    def each_swap(action):
        action(rcopy(grid_ref, gall.at[own_rows], ss_sem.at[0], g_sem.at[core], sib))

        @pl.when(core == 0)
        def _():
            action(rcopy(dsend_ref, dbuf.at[0, 0], ss_sem.at[1], i_sem.at[0], sib))
            action(rcopy(drecv_ref, dbuf.at[0, 1], ss_sem.at[4], i_sem.at[1], sib))
            action(rcopy(cot_ref, call.at[pl.ds(0, GRID)], ss_sem.at[2], c_sem.at[0], sib))

        @pl.when(core == 1)
        def _():
            action(rcopy(esend_ref, ebuf.at[1, 0], ss_sem.at[1], i_sem.at[2], sib))
            action(rcopy(erecv_ref, ebuf.at[1, 1], ss_sem.at[4], i_sem.at[3], sib))
            action(rcopy(lbuf.at[1], lbuf.at[1], ss_sem.at[5], i_sem.at[4], sib))

    each_halo((2,), lambda copy: copy.start())
    arrived(lone, own_sem.at[1])
    lbuf[core] = jnp.broadcast_to(lone[0], (8, 128))
    each_swap(lambda copy: copy.start())
    each_halo((0, 1), lambda copy: copy.start())

    @pl.when(jnp.logical_not(adjacent))
    def _():
        for role in (0, 1):
            for k in (3, 4, 5):
                fold[role, k] = jnp.zeros((NODES, D), BF16)

    def stage1_copies(mat, half):
        copies = []
        for step in (1, 3, 2):
            if half == 0:
                to = lax.rem(x + step, 4)
                dev = x_dev(to)
            else:
                to = lax.rem(y + step, 4)
                dev = y_dev(to)
            sem = (mat * 2 + half) * 3 + step - 1
            copies.append(
                rcopy(send1.at[mat, half, to], recv1.at[mat, half, step - 1], s1_sem.at[sem], r1_sem.at[sem], dev)
            )
        return copies

    def stage2_copies(mat, half):
        copies = []
        for step in (1, 3, 2):
            if half == 0:
                to = lax.rem(y + step, 4)
                dev = y_dev(to)
            else:
                to = lax.rem(x + step, 4)
                dev = x_dev(to)
            sem = (mat * 2 + half) * 3 + step - 1
            copies.append(
                rcopy(send2.at[mat, half, to], recv2.at[mat, half, step - 1], s2_sem.at[sem], r2_sem.at[sem], dev)
            )
        return copies

    def send_matrix(mat):
        for xx in range(4):
            pieces = []
            for yy in range(4):
                for zz in range(4):
                    row = ((yy // 2) * 4 + zz) * 64 + (yy % 2) * 32 + xx * 8
                    pieces.append(dwbuf[row : row + 8, 0:256])
            send1[mat, 0, xx] = jnp.concatenate(pieces, 0).astype(BF16)
        for yy in range(4):
            pieces = []
            for xx in range(4):
                for zz in range(4):
                    row = ((yy // 2) * 4 + zz) * 64 + (yy % 2) * 32 + xx * 8
                    pieces.append(dwbuf[row : row + 8, 256:512])
            send1[mat, 1, yy] = jnp.concatenate(pieces, 0).astype(BF16)
        for half in (0, 1):
            for copy in stage1_copies(mat, half):
                copy.start()

    def fold_copies(side, step):
        copies = []
        for which in ((0, 1) if side == 0 else (2,)):
            slot = ((yh + which) if side == 0 else cross_band) * 3 + 1 + step
            dev = (yh * 2 + which if side == 0 else (1 - yh) * 2 + yh, sector(step))
            rows = pl.ds(pl.multiple_of(slot * NODES, NODES), NODES)
            k = side * 3 + 1 - step
            copies.append(
                rcopy(part.at[rows], fold.at[core, k], fs_sem.at[which * 3 + step + 1], f_sem.at[core * 6 + k], dev)
            )
        return copies

    def each_fold(action):
        for step in (1, -1, 0):
            action(fold_copies(1, step)[0])
        for step in (1, -1):
            for copy in fold_copies(0, step):
                action(copy)
        to_first, to_second = fold_copies(0, 0)

        @pl.when(core == 0)
        def _():
            action(to_second)

        @pl.when(core == 1)
        def _():
            action(to_first)

    def gsum_copy():
        other = pl.ds(pl.multiple_of((1 - core) * GRID, GRID), GRID)
        return rcopy(gsum.at[other], gboth.at[core], ss_sem.at[3], gs_sem, sib)

    def weight(k):
        pltpu.make_async_copy(wts.at[k], wts.at[k], w_sem.at[k]).wait()

    def wait_band(band):
        for col in range(3):
            slot = band * 3 + col
            rows = pl.ds(pl.multiple_of(slot * NODES, NODES), NODES)
            arrived(mext.at[rows], m_sem.at[slot])

    def wait_cot(band):
        for col in range(3):
            slot = band * 3 + col
            rows = pl.ds(pl.multiple_of(slot * NODES, NODES), NODES)
            arrived(text.at[rows], t_sem.at[slot])

    def network(role):
        blocks = 2 if role == 0 else 3
        edges = blocks * 128
        w_grid, w_mesh = (0, 1) if role == 0 else (3, 2)
        for band in (0, 1):
            arrived(gall.at[pl.ds(band * GRID, GRID)], g_sem.at[band])
        weight(w_grid)
        gproj[...] = dot(gall[...], wts[w_grid]).astype(BF16)
        picks = ebuf if role == 0 else dbuf
        for band in (0, 1):
            for which in (0, 1):
                arrived(picks.at[band, which], i_sem.at[band * 2 + which])
        if role == 0:
            arrived(lbuf.at[1], i_sem.at[4])

        def rows_of(band, which):
            if role == 0:
                both = picks[band, which]
                return [both[q : q + 1] for q in range(blocks)]
            return [picks[band, which, q] for q in range(blocks)]

        grid_rows = [rows_of(b, role) for b in (0, 1)]
        mesh_rows = [[r + 192 * (yh + b - 1) for r in rows_of(b, 1 - role)] for b in (0, 1)]
        weight(4)
        for b in (0, 1):
            rows = slice(b * edges, (b + 1) * edges)
            g_pick = jnp.concatenate([pick_cols(r, GRID) for r in grid_rows[b]], 0)
            gpart[rows] = dot(g_pick, gproj[b * GRID : (b + 1) * GRID])
            if role == 1:
                arrived(call.at[pl.ds(b * GRID, GRID)], c_sem.at[b])
                picked = dot(g_pick, call[b * GRID : (b + 1) * GRID]).astype(BF16)
                msg[rows] = picked
                back[rows] = dot_bt(picked, wts[4])
        weight(w_mesh)
        for k in (0, 1, 2):
            band = (yh + k if k < 2 else cross_band)
            wait_band(band)
            rows = pl.ds(pl.multiple_of(band * 192, 192), 192)
            mproj[rows] = dot(mext[rows], wts[w_mesh]).astype(BF16)
        if role == 0:
            for band in range(3):
                wait_cot(band)
        for b in (0, 1):
            rows = slice(b * edges, (b + 1) * edges)
            m_pick = jnp.concatenate([pick_cols(r, EXT) for r in mesh_rows[b]], 0)
            pre = dot(m_pick, mproj[...]) + gpart[rows]
            if role == 0:
                place = lax.broadcasted_iota(I32, (edges, D), 0)
                live = lbuf[b, 0:1, 0:1]
                picked = jnp.where(place < live, dot(m_pick, text[...]), 0.0).astype(BF16)
                msg[rows] = picked
                grown = dot_bt(picked, wts[4])
            else:
                grown = back[rows]
            gate = 1.0 / (1.0 + jnp.exp(-pre))
            hid[rows] = (pre * gate).astype(BF16)
            pgrad[rows] = (grown * (gate * (1.0 + pre * (1.0 - gate)))).astype(BF16)
        every = slice(0, 2 * edges)
        dwbuf[...] = dot_at(hid[every], msg[every])
        send_matrix(2)
        m_turn = jnp.concatenate([pick_rows(r, EXT) for b in (0, 1) for r in mesh_rows[b]], 1)
        part[...] = dot(m_turn, pgrad[every]).astype(BF16)
        if role == 1:
            dwbuf[...] = dot_at(mext[...], part[...])
            send_matrix(0)
        for b in (0, 1):
            g_turn = jnp.concatenate([pick_rows(r, GRID) for r in grid_rows[b]], 1)
            gsum[b * GRID : (b + 1) * GRID] = dot(g_turn, pgrad[b * edges : (b + 1) * edges]).astype(BF16)
        gsum_copy().start()
        dwbuf[...] = dot_at(gall[...], gsum[...])
        send_matrix(0 if role == 0 else 1)
        if role == 0:
            dwbuf[...] = dot_at(mext[...], part[...])
            send_matrix(1)

    @pl.when(core == 0)
    def _():
        network(0)

    @pl.when(core == 1)
    def _():
        network(1)

    @pl.when(core == 0)
    def _():
        for k in (2, 3):
            weight(k)
        arrived(call.at[own_rows], c_sem.at[0])

    @pl.when(core == 1)
    def _():
        for k in (0, 1):
            weight(k)

    arrived(town, own_sem.at[0])

    for mat in (2, 0, 1):
        for half in (0, 1):
            for step in range(3):
                sem = (mat * 2 + half) * 3 + step
                arrived(recv1.at[mat, half, step], r1_sem.at[sem])
            own = x if half == 0 else y
            total = send1[mat, half, own].astype(F32)
            for step in range(3):
                total = total + recv1[mat, half, step].astype(F32)
            total = total.astype(BF16)
            for k in range(4):
                send2[mat, half, k] = total[k * 32 : (k + 1) * 32]
            for copy in stage2_copies(mat, half):
                copy.start()

    each_fold(lambda copy: copy.start())

    gboth[core] = gsum[own_rows]
    arrived(gboth.at[1 - core], gs_sem)
    grid_out[...] = (call[own_rows].astype(F32) + dot_bt(gboth[0], wts[0]) + dot_bt(gboth[1], wts[3])).astype(BF16)

    sums = []
    for mat in range(3):
        for half in (0, 1):
            for step in range(3):
                sem = (mat * 2 + half) * 3 + step
                arrived(recv2.at[mat, half, step], r2_sem.at[sem])
            own = y if half == 0 else x
            total = send2[mat, half, own].astype(F32)
            for step in range(3):
                total = total + recv2[mat, half, step].astype(F32)
            sums.append(total)
    for q in range(4):
        send3[q] = jnp.concatenate([s[q * 8 : (q + 1) * 8] for s in sums], 0).astype(BF16)

    holds = lax.div(z, 4) == yh

    def stage3_copy(step):
        to = lax.rem(z + step, 8)
        return (
            lax.div(to, 4) == yh,
            rcopy(send3.at[lax.rem(to, 4)], recv3.at[step - 1], s3_sem.at[step - 1], r3_sem.at[step - 1], z_dev(to)),
        )

    for step in (4, 3, 5, 2, 6, 1, 7):
        goes, copy = stage3_copy(step)
        pl.when(goes)(copy.start)

    def part_of(slot):
        return pl.ds(pl.multiple_of(slot * NODES, NODES), NODES)

    def fold_wait(role, k):
        arrived(fold.at[role, k], f_sem.at[role * 6 + k])

    for role in (0, 1):
        for k in (0, 2):
            fold_wait(role, k)
    own_slot = part_of((yh + core) * 3 + 1)

    @pl.when(core == 0)
    def _():
        fold_wait(1, 1)
        fold[0, 1] = part[own_slot]

    @pl.when(core == 1)
    def _():
        fold_wait(0, 1)
        fold[1, 1] = part[own_slot]

    @pl.when(adjacent)
    def _():
        for role in (0, 1):
            for k in (3, 4, 5):
                fold_wait(role, k)

    def folded(role):
        total = fold[role, 0].astype(F32)
        for k in range(1, 6):
            total = total + fold[role, k].astype(F32)
        return total.astype(BF16)

    mesh_out[...] = (town[...].astype(F32) + dot_bt(folded(0), wts[1])).astype(BF16)
    proc_out[...] = dot_bt(folded(1), wts[2]).astype(BF16)

    def last_copies():
        devs = (((1 - yh) * 2 + core, lon), ((1 - yh) * 2 + 1 - core, lon), sib)
        return [rcopy(final.at[core], final.at[core], s4_sem.at[k], r4_sem.at[core], dev) for k, dev in enumerate(devs)]

    @pl.when(holds)
    def _():
        total = send3[lax.rem(z, 4)].astype(F32)
        for step in (1, 7, 2, 6, 3, 5, 4):
            arrived(recv3.at[step - 1], r3_sem.at[step - 1])
            total = total + recv3[step - 1].astype(F32)
        final[core] = (total * grad_scale).astype(BF16)
        for copy in last_copies():
            copy.start()
        arrived(final.at[1 - core], r4_sem.at[1 - core])

    @pl.when(jnp.logical_not(holds))
    def _():
        arrived(final.at[0], r4_sem.at[0])
        arrived(final.at[1], r4_sem.at[1])

    for role in (0, 1):
        pieces = final[role].astype(F32)
        for mat in range(3):
            weights_out[role, mat, :, 0:256] = pieces[mat * 16 : mat * 16 + 8]
            weights_out[role, mat, :, 256:512] = pieces[mat * 16 + 8 : mat * 16 + 16]

    each_swap(lambda copy: copy.wait_send())
    each_halo((2,), lambda copy: copy.wait_send())
    each_halo((0, 1), lambda copy: copy.wait_send())
    each_fold(lambda copy: copy.wait_send())

    gsum_copy().wait_send()
    for mat in range(3):
        for half in (0, 1):
            for copy in stage1_copies(mat, half) + stage2_copies(mat, half):
                copy.wait_send()
    for step in range(1, 8):
        goes, copy = stage3_copy(step)
        pl.when(goes)(copy.wait_send)

    @pl.when(holds)
    def _():
        for copy in last_copies():
            copy.wait_send()


def write_out(grid_in, mesh_in, proc_in, weights_in, grid_out, mesh_out, proc_out, enc_out, dec_out, sem):
    copies = [
        pltpu.make_async_copy(grid_in, grid_out.at[0, 0], sem.at[0]),
        pltpu.make_async_copy(mesh_in, mesh_out.at[0, 0], sem.at[1]),
        pltpu.make_async_copy(proc_in, proc_out.at[0, 0], sem.at[2]),
        pltpu.make_async_copy(weights_in.at[0], enc_out, sem.at[3]),
        pltpu.make_async_copy(weights_in.at[1], dec_out, sem.at[4]),
    ]
    for copy in copies:
        copy.start()
    for copy in copies:
        copy.wait()


def shards(
    grid_latent,
    grid_cot,
    mesh_latent,
    mesh_cot,
    processed,
    enc_weights,
    dec_weights,
    enc_send,
    enc_recv,
    enc_live,
    dec_send,
    dec_recv,
):
    grad_scale = 1.0 / math.sqrt(4 * 64 * 128)
    vmem = pltpu.VMEM
    dma = pltpu.SemaphoreType.DMA
    outs = pl.pallas_call(
        lambda *refs: kernel(*refs, grad_scale),
        out_shape=(
            jax.ShapeDtypeStruct((GRID, D), BF16),
            jax.ShapeDtypeStruct((NODES, D), BF16),
            jax.ShapeDtypeStruct((NODES, D), BF16),
            jax.ShapeDtypeStruct((2, 3, 8, D), F32),
        ),
        in_specs=[pl.BlockSpec(memory_space=pltpu.HBM)] * 12,
        out_specs=(pl.BlockSpec(memory_space=pltpu.VMEM),) * 4,
        scratch_shapes=[
            vmem((5, D, D), BF16),
            vmem((2 * GRID, D), BF16),
            vmem((2 * GRID, D), BF16),
            vmem((EXT, D), BF16),
            vmem((EXT, D), BF16),
            vmem((NODES, D), BF16),
            vmem((2, 2, 2, 128), I32),
            vmem((2, 2, 3, 1, 128), I32),
            vmem((2, 8, 128), I32),
            vmem((1, 1, 1), I32),
            vmem((2 * GRID, D), BF16),
            vmem((EXT, D), BF16),
            vmem((768, D), F32),
            vmem((768, D), F32),
            vmem((768, D), BF16),
            vmem((768, D), BF16),
            vmem((768, D), BF16),
            vmem((EXT, D), BF16),
            vmem((2 * GRID, D), BF16),
            vmem((2, GRID, D), BF16),
            vmem((2, 6, NODES, D), BF16),
            vmem((D, D), F32),
            vmem((3, 2, 4, 128, 256), BF16),
            vmem((3, 2, 3, 128, 256), BF16),
            vmem((3, 2, 4, 32, 256), BF16),
            vmem((3, 2, 3, 32, 256), BF16),
            vmem((4, 48, 256), BF16),
            vmem((7, 48, 256), BF16),
            vmem((2, 48, 256), BF16),
            dma((5,)),
            dma((2,)),
            dma((5,)),
            dma((2,)),
            dma((2,)),
            dma((9,)),
            dma((9,)),
            dma((12,)),
            dma,
            dma((18,)),
            dma((18,)),
            dma((7,)),
            dma((2,)),
            dma((18,)),
            dma((6,)),
            dma((9,)),
            dma((18,)),
            dma((18,)),
            dma((7,)),
            dma((3,)),
        ],
        compiler_params=pltpu.CompilerParams(
            collective_id=0, has_side_effects=True, vmem_limit_bytes=48 * 2**20
        ),
        name="edge_layer",
    )(
        *(
            array if array is enc_live else pltpu.with_memory_space_constraint(array, pltpu.HBM)
            for array in (
                grid_latent[0, 0],
                grid_cot[0, 0],
                mesh_latent[0, 0],
                mesh_cot[0, 0],
                processed[0, 0],
                enc_weights,
                dec_weights,
                enc_send[0, 0],
                enc_recv[0, 0],
                enc_live,
                dec_send.reshape(3, 1, 128),
                dec_recv.reshape(3, 1, 128),
            )
        )
    )
    return pl.pallas_call(
        write_out,
        out_shape=(
            jax.ShapeDtypeStruct((1, 1, GRID, D), BF16),
            jax.ShapeDtypeStruct((1, 1, NODES, D), BF16),
            jax.ShapeDtypeStruct((1, 1, NODES, D), BF16),
            jax.ShapeDtypeStruct((3, 8, D), F32),
            jax.ShapeDtypeStruct((3, 8, D), F32),
        ),
        in_specs=[pl.BlockSpec(memory_space=pltpu.VMEM)] * 4,
        out_specs=(pl.BlockSpec(memory_space=pltpu.HBM),) * 5,
        scratch_shapes=[dma((5,))],
        compiler_params=pltpu.CompilerParams(vmem_limit_bytes=2 * 2**20),
        name="write_out",
    )(*(pltpu.with_memory_space_constraint(array, pltpu.VMEM) for array in outs))


def solution(mesh):
    by_node = P("lat", "lon", None, None)
    return jax.shard_map(
        shards,
        mesh=mesh,
        in_specs=(by_node,) * 5 + (P(), P()) + (by_node, by_node, P("lat", "lon", None), by_node, by_node),
        out_specs=(by_node, by_node, by_node, P(None, "lon", None), P(None, "lon", None)),
        check_vma=False,
    )
```

```python
import math

import jax
import jax.numpy as jnp
from jax import lax
from jax.experimental import pallas as pl
from jax.experimental.pallas import tpu as pltpu
from jax.sharding import PartitionSpec as P

BF16 = jnp.bfloat16
F32 = jnp.float32
I32 = jnp.int32
MESH = pl.DeviceIdType.MESH
D = 512
GRID = 128
NODES = 64
SLOTS = 9
EXT = SLOTS * NODES


def dot(a, b):
    return lax.dot_general(a, b, (((1,), (0,)), ((), ())), preferred_element_type=F32)


def dot_bt(a, b):
    return lax.dot_general(a, b, (((1,), (1,)), ((), ())), preferred_element_type=F32)


def dot_at(a, b):
    return lax.dot_general(a, b, (((0,), (0,)), ((), ())), preferred_element_type=F32)


def pick_rows(index_row, rows):
    return jnp.where(lax.broadcasted_iota(I32, (rows, 128), 0) == index_row, 1.0, 0.0).astype(BF16)


def pick_cols(index_row, columns):
    turned = jnp.transpose(jnp.broadcast_to(index_row, (128, 128)))
    lane = lax.broadcasted_iota(I32, (128, 128), 1)
    parts = []
    for start in range(0, columns, 128):
        part = jnp.where(turned == lane + start, 1.0, 0.0).astype(BF16)
        parts.append(part[:, : min(128, columns - start)])
    return parts[0] if len(parts) == 1 else jnp.concatenate(parts, 1)


def kernel(
    grid_ref,
    cot_ref,
    mesh_ref,
    mcot_ref,
    proc_ref,
    encw_ref,
    decw_ref,
    esend_ref,
    erecv_ref,
    live_ref,
    dsend_ref,
    drecv_ref,
    grid_out,
    mesh_out,
    proc_out,
    weights_out,
    wts,
    gall,
    call,
    mext,
    text,
    town,
    ebuf,
    dbuf,
    lbuf,
    lone,
    gproj,
    mproj,
    gpart,
    back,
    hid,
    msg,
    pgrad,
    part,
    gsum,
    gboth,
    fold,
    dwbuf,
    send1,
    recv1,
    send2,
    recv2,
    send3,
    recv3,
    final,
    zsend,
    zrecv,
    xsend,
    xrecv,
    ysend,
    yrecv,
    last,
    w_sem,
    own_sem,
    i_sem,
    g_sem,
    c_sem,
    m_sem,
    t_sem,
    f_sem,
    gs_sem,
    r1_sem,
    r2_sem,
    r3_sem,
    r4_sem,
    hs_sem,
    ss_sem,
    fs_sem,
    s1_sem,
    s2_sem,
    s3_sem,
    s4_sem,
    zs_sem,
    zr_sem,
    xs_sem,
    xr_sem,
    ys_sem,
    yr_sem,
    ls_sem,
    lr_sem,
    grad_scale,
):
    lat = lax.axis_index("lat")
    lon = lax.axis_index("lon")
    yh = lax.div(lat, 2)
    core = lax.rem(lat, 2)
    z = lax.div(lon, 8)
    yl = lax.rem(lax.div(lon, 4), 2)
    x = lax.rem(lon, 4)
    y = yh * 2 + yl
    sib = (yh * 2 + (1 - core), lon)
    adjacent = core == 1 - yh

    def lon_of(zz, yy, xx):
        return zz * 8 + yy * 4 + xx

    def sector(step):
        return lax.rem(lon + step + 64, 64)

    def x_dev(xx):
        return (lat, lon_of(z, yl, xx))

    def y_dev(yy):
        return (lax.div(yy, 2) * 2 + core, lon_of(z, lax.rem(yy, 2), x))

    def z_dev(zz):
        return (lat, lon_of(zz, yl, x))

    def rcopy(src, dst, ssem, rsem, dev):
        return pltpu.make_async_remote_copy(
            src_ref=src, dst_ref=dst, send_sem=ssem, recv_sem=rsem, device_id=dev, device_id_type=MESH
        )

    def arrived(dst, rsem):
        pltpu.make_async_copy(dst, dst, rsem).wait()

    def load(src, dst, sem):
        pltpu.make_async_copy(src, dst, sem).start()

    load(encw_ref.at[0], wts.at[0], w_sem.at[0])
    load(decw_ref.at[1], wts.at[3], w_sem.at[3])
    load(encw_ref.at[1], wts.at[1], w_sem.at[1])
    load(decw_ref.at[0], wts.at[2], w_sem.at[2])

    @pl.when(core == 0)
    def _():
        load(encw_ref.at[2], wts.at[4], w_sem.at[4])
        load(esend_ref, ebuf.at[0, 0], i_sem.at[0])
        load(erecv_ref, ebuf.at[0, 1], i_sem.at[1])
        load(mesh_ref, mext.at[pl.ds(pl.multiple_of((yh * 3 + 1) * NODES, NODES), NODES)], m_sem.at[yh * 3 + 1])
        load(mcot_ref, text.at[pl.ds(pl.multiple_of((yh * 3 + 1) * NODES, NODES), NODES)], t_sem.at[yh * 3 + 1])

    @pl.when(core == 1)
    def _():
        load(decw_ref.at[2], wts.at[4], w_sem.at[4])
        load(dsend_ref, dbuf.at[1, 0], i_sem.at[2])
        load(drecv_ref, dbuf.at[1, 1], i_sem.at[3])
        slot = (yh + 1) * 3 + 1
        load(proc_ref, mext.at[pl.ds(pl.multiple_of(slot * NODES, NODES), NODES)], m_sem.at[slot])

    own_rows = pl.ds(pl.multiple_of(core * GRID, GRID), GRID)
    load(grid_ref, gall.at[own_rows], g_sem.at[core])
    load(cot_ref, call.at[own_rows], c_sem.at[core])
    load(mcot_ref, town, own_sem.at[0])
    load(live_ref, lone, own_sem.at[1])

    barrier = pltpu.get_barrier_semaphore()
    greeted = []
    for dyh in (0, 1):
        for dc in (0, 1):
            for step in (-1, 0, 1):
                if (dyh, dc, step) != (0, 0, 0):
                    to_yh = yh if dyh == 0 else 1 - yh
                    to_core = core if dc == 0 else 1 - core
                    greeted.append((to_yh * 2 + to_core, sector(step)))
    for step in range(1, 4):
        greeted.append(x_dev(lax.rem(x + step, 4)))
        greeted.append(y_dev(lax.rem(y + step, 4)))
    for step in range(1, 8):
        greeted.append(z_dev(lax.rem(z + step, 8)))
    for dev in greeted:
        pl.semaphore_signal(barrier, inc=1, device_id=dev, device_id_type=MESH)
    pl.semaphore_wait(barrier, len(greeted))

    def halo_copy(which, side, step):
        to_yh = yh if side == 0 else 1 - yh
        slot = (lat - to_yh) * 3 + 1 - step
        rows = pl.ds(pl.multiple_of(slot * NODES, NODES), NODES)
        at = side * 9 + (step + 1) * 3
        enc_dev = (to_yh * 2, sector(step))
        dec_dev = (to_yh * 2 + 1, sector(step))
        if which == 0:
            return rcopy(mesh_ref, mext.at[rows], hs_sem.at[at], m_sem.at[slot], enc_dev)
        if which == 1:
            return rcopy(mcot_ref, text.at[rows], hs_sem.at[at + 1], t_sem.at[slot], enc_dev)
        return rcopy(proc_ref, mext.at[rows], hs_sem.at[at + 2], m_sem.at[slot], dec_dev)

    def each_halo(which, action):
        @pl.when(adjacent)
        def _():
            for step in (1, -1, 0):
                action(halo_copy(which, 1, step))

        for step in (1, -1):
            action(halo_copy(which, 0, step))

        @pl.when(core == (0 if which == 2 else 1))
        def _():
            action(halo_copy(which, 0, 0))

    cross_band = 2 - 2 * yh

    def each_swap(action):
        action(rcopy(grid_ref, gall.at[own_rows], ss_sem.at[0], g_sem.at[core], sib))

        @pl.when(core == 0)
        def _():
            action(rcopy(dsend_ref, dbuf.at[0, 0], ss_sem.at[1], i_sem.at[0], sib))
            action(rcopy(drecv_ref, dbuf.at[0, 1], ss_sem.at[4], i_sem.at[1], sib))
            action(rcopy(cot_ref, call.at[pl.ds(0, GRID)], ss_sem.at[2], c_sem.at[0], sib))

        @pl.when(core == 1)
        def _():
            action(rcopy(esend_ref, ebuf.at[1, 0], ss_sem.at[1], i_sem.at[2], sib))
            action(rcopy(erecv_ref, ebuf.at[1, 1], ss_sem.at[4], i_sem.at[3], sib))
            action(rcopy(lbuf.at[1], lbuf.at[1], ss_sem.at[5], i_sem.at[4], sib))

    each_halo(2, lambda copy: copy.start())
    each_halo(0, lambda copy: copy.start())
    arrived(lone, own_sem.at[1])
    lbuf[core] = jnp.broadcast_to(lone[0], (8, 128))
    each_swap(lambda copy: copy.start())
    each_halo(1, lambda copy: copy.start())

    @pl.when(jnp.logical_not(adjacent))
    def _():
        for role in (0, 1):
            for k in (3, 4, 5):
                fold[role, k] = jnp.zeros((NODES, D), BF16)

    def stage1_copies(mat, half):
        copies = []
        for step in (1, 3, 2):
            if half == 0:
                to = lax.rem(x + step, 4)
                dev = x_dev(to)
            else:
                to = lax.rem(y + step, 4)
                dev = y_dev(to)
            sem = (mat * 2 + half) * 3 + step - 1
            copies.append(
                rcopy(send1.at[mat, half, to], recv1.at[mat, half, step - 1], s1_sem.at[sem], r1_sem.at[sem], dev)
            )
        return copies

    def stage2_copies(mat, half):
        copies = []
        for step in (1, 3, 2):
            if half == 0:
                to = lax.rem(y + step, 4)
                dev = y_dev(to)
            else:
                to = lax.rem(x + step, 4)
                dev = x_dev(to)
            sem = (mat * 2 + half) * 3 + step - 1
            copies.append(
                rcopy(send2.at[mat, half, to], recv2.at[mat, half, step - 1], s2_sem.at[sem], r2_sem.at[sem], dev)
            )
        return copies

    def send_matrix(mat):
        for xx in range(4):
            pieces = []
            for yy in range(4):
                for zz in range(4):
                    row = ((yy // 2) * 4 + zz) * 64 + (yy % 2) * 32 + xx * 8
                    pieces.append(dwbuf[row : row + 8, 0:256])
            send1[mat, 0, xx] = jnp.concatenate(pieces, 0).astype(BF16)
        for yy in range(4):
            pieces = []
            for xx in range(4):
                for zz in range(4):
                    row = ((yy // 2) * 4 + zz) * 64 + (yy % 2) * 32 + xx * 8
                    pieces.append(dwbuf[row : row + 8, 256:512])
            send1[mat, 1, yy] = jnp.concatenate(pieces, 0).astype(BF16)
        for half in (0, 1):
            for copy in stage1_copies(mat, half):
                copy.start()

    def z_copies():
        copies = []
        for step in (4, 3, 5, 2, 6, 1, 7):
            to = lax.rem(z + step, 8)
            copies.append(rcopy(zsend.at[to], zrecv.at[step - 1], zs_sem.at[step - 1], zr_sem.at[step - 1], z_dev(to)))
        return copies

    def x_copies():
        copies = []
        for step in (2, 1, 3):
            to = lax.rem(x + step, 4)
            copies.append(rcopy(xsend.at[to], xrecv.at[step - 1], xs_sem.at[step - 1], xr_sem.at[step - 1], x_dev(to)))
        return copies

    def y_copies():
        copies = []
        for step in (2, 1, 3):
            to = lax.rem(y + step, 4)
            copies.append(rcopy(ysend.at[lax.rem(to, 2)], yrecv.at[y], ys_sem.at[step - 1], yr_sem.at[y], y_dev(to)))
        return copies

    def sibling_copy():
        return rcopy(last.at[core], last.at[core], ls_sem, lr_sem, sib)

    def send_out_matrix():
        for zz in range(8):
            zsend[zz] = dwbuf[zz * 64 : (zz + 1) * 64].astype(BF16)
        for copy in z_copies():
            copy.start()

    def fold_copies(side, step):
        copies = []
        for which in ((0, 1) if side == 0 else (2,)):
            slot = ((yh + which) if side == 0 else cross_band) * 3 + 1 + step
            dev = (yh * 2 + which if side == 0 else (1 - yh) * 2 + yh, sector(step))
            rows = pl.ds(pl.multiple_of(slot * NODES, NODES), NODES)
            k = side * 3 + 1 - step
            copies.append(
                rcopy(part.at[rows], fold.at[core, k], fs_sem.at[which * 3 + step + 1], f_sem.at[core * 6 + k], dev)
            )
        return copies

    def each_fold(role, action):
        for step in (1, -1, 0):
            action(fold_copies(1, step)[0])
        for step in (1, -1):
            for copy in fold_copies(0, step):
                action(copy)
        action(fold_copies(0, 0)[1 - role])

    def gsum_copy():
        other = pl.ds(pl.multiple_of((1 - core) * GRID, GRID), GRID)
        return rcopy(gsum.at[other], gboth.at[core], ss_sem.at[3], gs_sem, sib)

    def weight(k):
        pltpu.make_async_copy(wts.at[k], wts.at[k], w_sem.at[k]).wait()

    def wait_band(band):
        for col in range(3):
            slot = band * 3 + col
            rows = pl.ds(pl.multiple_of(slot * NODES, NODES), NODES)
            arrived(mext.at[rows], m_sem.at[slot])

    def wait_cot(band):
        for col in range(3):
            slot = band * 3 + col
            rows = pl.ds(pl.multiple_of(slot * NODES, NODES), NODES)
            arrived(text.at[rows], t_sem.at[slot])

    def network(role):
        blocks = 2 if role == 0 else 3
        edges = blocks * 128
        w_grid, w_mesh = (0, 1) if role == 0 else (3, 2)
        for band in (0, 1):
            arrived(gall.at[pl.ds(band * GRID, GRID)], g_sem.at[band])
        weight(w_grid)
        gproj[...] = dot(gall[...], wts[w_grid]).astype(BF16)
        picks = ebuf if role == 0 else dbuf
        for band in (0, 1):
            for which in (0, 1):
                arrived(picks.at[band, which], i_sem.at[band * 2 + which])
        if role == 0:
            arrived(lbuf.at[1], i_sem.at[4])

        def rows_of(band, which):
            if role == 0:
                both = picks[band, which]
                return [both[q : q + 1] for q in range(blocks)]
            return [picks[band, which, q] for q in range(blocks)]

        grid_rows = [rows_of(b, role) for b in (0, 1)]
        mesh_rows = [[r + 192 * (yh + b - 1) for r in rows_of(b, 1 - role)] for b in (0, 1)]
        weight(4)
        for b in (0, 1):
            rows = slice(b * edges, (b + 1) * edges)
            g_pick = jnp.concatenate([pick_cols(r, GRID) for r in grid_rows[b]], 0)
            gpart[rows] = dot(g_pick, gproj[b * GRID : (b + 1) * GRID])
            if role == 1:
                arrived(call.at[pl.ds(b * GRID, GRID)], c_sem.at[b])
                picked = dot(g_pick, call[b * GRID : (b + 1) * GRID]).astype(BF16)
                msg[rows] = picked
                back[rows] = dot_bt(picked, wts[4])
        weight(w_mesh)
        for k in (0, 1, 2):
            band = (yh + k if k < 2 else cross_band)
            wait_band(band)
            rows = pl.ds(pl.multiple_of(band * 192, 192), 192)
            mproj[rows] = dot(mext[rows], wts[w_mesh]).astype(BF16)
        m_picks = []
        for b in (0, 1):
            rows = slice(b * edges, (b + 1) * edges)
            m_picks.append(jnp.concatenate([pick_cols(r, EXT) for r in mesh_rows[b]], 0))
            pre = dot(m_picks[b], mproj[...]) + gpart[rows]
            gate = 1.0 / (1.0 + jnp.exp(-pre))
            hid[rows] = (pre * gate).astype(BF16)
            gpart[rows] = gate * (1.0 + pre * (1.0 - gate))
        if role == 0:
            for band in range(3):
                wait_cot(band)
            for b in (0, 1):
                rows = slice(b * edges, (b + 1) * edges)
                place = lax.broadcasted_iota(I32, (edges, D), 0)
                live = lbuf[b, 0:1, 0:1]
                picked = jnp.where(place < live, dot(m_picks[b], text[...]), 0.0).astype(BF16)
                msg[rows] = picked
                back[rows] = dot_bt(picked, wts[4])
        every = slice(0, 2 * edges)
        dwbuf[...] = dot_at(hid[every], msg[every])
        send_out_matrix()
        pgrad[every] = (back[every] * gpart[every]).astype(BF16)
        m_turn = jnp.concatenate([pick_rows(r, EXT) for b in (0, 1) for r in mesh_rows[b]], 1)
        part[...] = dot(m_turn, pgrad[every]).astype(BF16)
        if role == 1:
            each_fold(1, lambda copy: copy.start())
            dwbuf[...] = dot_at(mext[...], part[...])
            send_matrix(0)
        for b in (0, 1):
            g_turn = jnp.concatenate([pick_rows(r, GRID) for r in grid_rows[b]], 1)
            gsum[b * GRID : (b + 1) * GRID] = dot(g_turn, pgrad[b * edges : (b + 1) * edges]).astype(BF16)
        gsum_copy().start()
        dwbuf[...] = dot_at(gall[...], gsum[...])
        send_matrix(0 if role == 0 else 1)
        if role == 0:
            dwbuf[...] = dot_at(mext[...], part[...])
            send_matrix(1)

    @pl.when(core == 0)
    def _():
        network(0)

    @pl.when(core == 1)
    def _():
        network(1)

    @pl.when(core == 0)
    def _():
        for k in (2, 3):
            weight(k)
        arrived(call.at[own_rows], c_sem.at[0])

    @pl.when(core == 1)
    def _():
        for k in (0, 1):
            weight(k)

    arrived(town, own_sem.at[0])

    for mat in (0, 1):
        for half in (0, 1):
            for step in range(3):
                sem = (mat * 2 + half) * 3 + step
                arrived(recv1.at[mat, half, step], r1_sem.at[sem])
            own = x if half == 0 else y
            total = send1[mat, half, own].astype(F32)
            for step in range(3):
                total = total + recv1[mat, half, step].astype(F32)
            total = total.astype(BF16)
            for k in range(4):
                send2[mat, half, k] = total[k * 32 : (k + 1) * 32]
            for copy in stage2_copies(mat, half):
                copy.start()

    total = zsend[z].astype(F32)
    for step in range(1, 8):
        arrived(zrecv.at[step - 1], zr_sem.at[step - 1])
        total = total + zrecv[step - 1].astype(F32)
    for xx in range(4):
        xsend[xx] = jnp.concatenate([total[xx * 8 : xx * 8 + 8], total[32 + xx * 8 : 40 + xx * 8]], 0).astype(BF16)
    for copy in x_copies():
        copy.start()

    holds = lax.div(z, 4) == yh

    def each_stage3(mat, action):
        for step in (4, 3, 5, 2, 6, 1, 7):
            to = lax.rem(z + step, 8)

            @pl.when(lax.div(to, 4) == yh)
            def _():
                sem = mat * 7 + step - 1
                action(
                    rcopy(send3.at[mat, lax.rem(to, 4)], recv3.at[mat, step - 1], s3_sem.at[sem], r3_sem.at[sem], z_dev(to))
                )

    def stage3(mat):
        sums = []
        for half in (0, 1):
            for step in range(3):
                sem = (mat * 2 + half) * 3 + step
                arrived(recv2.at[mat, half, step], r2_sem.at[sem])
            own = y if half == 0 else x
            total = send2[mat, half, own].astype(F32)
            for step in range(3):
                total = total + recv2[mat, half, step].astype(F32)
            sums.append(total)
        for q in range(4):
            send3[mat, q] = jnp.concatenate([t[q * 8 : (q + 1) * 8] for t in sums], 0).astype(BF16)
        each_stage3(mat, lambda copy: copy.start())

    stage3(0)

    @pl.when(core == 0)
    def _():
        each_fold(0, lambda copy: copy.start())

    stage3(1)

    total = xsend[x].astype(F32)
    for step in range(1, 4):
        arrived(xrecv.at[step - 1], xr_sem.at[step - 1])
        total = total + xrecv[step - 1].astype(F32)
    ysend[0] = total[0:8]
    ysend[1] = total[8:16]
    for copy in y_copies():
        copy.start()

    gboth[core] = gsum[own_rows]
    arrived(gboth.at[1 - core], gs_sem)
    grid_out[...] = (call[own_rows].astype(F32) + dot_bt(gboth[0], wts[0]) + dot_bt(gboth[1], wts[3])).astype(BF16)

    def last_copies():
        devs = (((1 - yh) * 2 + core, lon), ((1 - yh) * 2 + 1 - core, lon), sib)
        return [rcopy(final.at[core], final.at[core], s4_sem.at[k], r4_sem.at[core], dev) for k, dev in enumerate(devs)]

    @pl.when(holds)
    def _():
        totals = []
        for mat in (0, 1):
            for step in range(1, 8):
                arrived(recv3.at[mat, step - 1], r3_sem.at[mat * 7 + step - 1])
        for mat in (0, 1):
            total = send3[mat, lax.rem(z, 4)].astype(F32)
            for step in range(1, 8):
                total = total + recv3[mat, step - 1].astype(F32)
            totals.append(total)
        total = jnp.concatenate(totals, 0)
        final[core] = (total * grad_scale).astype(BF16)
        for copy in last_copies():
            copy.start()

    yrecv[y] = ysend[yl]
    for step in (1, 3, 2):
        beyond = lax.rem(y + step, 4)
        arrived(yrecv.at[beyond], yr_sem.at[beyond])
    last[core] = (yrecv[0] + yrecv[1] + yrecv[2] + yrecv[3]) * grad_scale
    sibling_copy().start()

    def part_of(slot):
        return pl.ds(pl.multiple_of(slot * NODES, NODES), NODES)

    def fold_wait(role, k):
        arrived(fold.at[role, k], f_sem.at[role * 6 + k])

    for role in (0, 1):
        for k in (0, 2):
            fold_wait(role, k)
    own_slot = part_of((yh + core) * 3 + 1)

    @pl.when(core == 0)
    def _():
        fold_wait(1, 1)
        fold[0, 1] = part[own_slot]

    @pl.when(core == 1)
    def _():
        fold_wait(0, 1)
        fold[1, 1] = part[own_slot]

    @pl.when(adjacent)
    def _():
        for role in (0, 1):
            for k in (3, 4, 5):
                fold_wait(role, k)

    def folded(role):
        total = fold[role, 0].astype(F32)
        for k in range(1, 6):
            total = total + fold[role, k].astype(F32)
        return total.astype(BF16)

    mesh_out[...] = (town[...].astype(F32) + dot_bt(folded(0), wts[1])).astype(BF16)
    proc_out[...] = dot_bt(folded(1), wts[2]).astype(BF16)

    @pl.when(holds)
    def _():
        arrived(final.at[1 - core], r4_sem.at[1 - core])

    @pl.when(jnp.logical_not(holds))
    def _():
        arrived(final.at[0], r4_sem.at[0])
        arrived(final.at[1], r4_sem.at[1])

    arrived(last.at[1 - core], lr_sem)
    for role in (0, 1):
        pieces = final[role].astype(F32)
        weights_out[role, 2] = last[role]
        for mat in (0, 1):
            weights_out[role, mat, :, 0:256] = pieces[mat * 16 : mat * 16 + 8]
            weights_out[role, mat, :, 256:512] = pieces[mat * 16 + 8 : mat * 16 + 16]

    each_swap(lambda copy: copy.wait_send())
    for which in range(3):
        each_halo(which, lambda copy: copy.wait_send())
    @pl.when(core == 0)
    def _():
        each_fold(0, lambda copy: copy.wait_send())

    @pl.when(core == 1)
    def _():
        each_fold(1, lambda copy: copy.wait_send())


    gsum_copy().wait_send()
    for copy in z_copies() + x_copies() + y_copies() + [sibling_copy()]:
        copy.wait_send()
    for mat in (0, 1):
        for half in (0, 1):
            for copy in stage1_copies(mat, half) + stage2_copies(mat, half):
                copy.wait_send()
    for mat in (0, 1):
        each_stage3(mat, lambda copy: copy.wait_send())

    @pl.when(holds)
    def _():
        for copy in last_copies():
            copy.wait_send()


def write_out(grid_in, mesh_in, proc_in, weights_in, grid_out, mesh_out, proc_out, enc_out, dec_out, sem):
    copies = [
        pltpu.make_async_copy(grid_in, grid_out.at[0, 0], sem.at[0]),
        pltpu.make_async_copy(mesh_in, mesh_out.at[0, 0], sem.at[1]),
        pltpu.make_async_copy(proc_in, proc_out.at[0, 0], sem.at[2]),
        pltpu.make_async_copy(weights_in.at[0], enc_out, sem.at[3]),
        pltpu.make_async_copy(weights_in.at[1], dec_out, sem.at[4]),
    ]
    for copy in copies:
        copy.start()
    for copy in copies:
        copy.wait()


def shards(
    grid_latent,
    grid_cot,
    mesh_latent,
    mesh_cot,
    processed,
    enc_weights,
    dec_weights,
    enc_send,
    enc_recv,
    enc_live,
    dec_send,
    dec_recv,
):
    grad_scale = 1.0 / math.sqrt(4 * 64 * 128)
    vmem = pltpu.VMEM
    dma = pltpu.SemaphoreType.DMA
    outs = pl.pallas_call(
        lambda *refs: kernel(*refs, grad_scale),
        out_shape=(
            jax.ShapeDtypeStruct((GRID, D), BF16),
            jax.ShapeDtypeStruct((NODES, D), BF16),
            jax.ShapeDtypeStruct((NODES, D), BF16),
            jax.ShapeDtypeStruct((2, 3, 8, D), F32),
        ),
        in_specs=[pl.BlockSpec(memory_space=pltpu.HBM)] * 12,
        out_specs=(pl.BlockSpec(memory_space=pltpu.VMEM),) * 4,
        scratch_shapes=[
            vmem((5, D, D), BF16),
            vmem((2 * GRID, D), BF16),
            vmem((2 * GRID, D), BF16),
            vmem((EXT, D), BF16),
            vmem((EXT, D), BF16),
            vmem((NODES, D), BF16),
            vmem((2, 2, 2, 128), I32),
            vmem((2, 2, 3, 1, 128), I32),
            vmem((2, 8, 128), I32),
            vmem((1, 1, 1), I32),
            vmem((2 * GRID, D), BF16),
            vmem((EXT, D), BF16),
            vmem((768, D), F32),
            vmem((768, D), F32),
            vmem((768, D), BF16),
            vmem((768, D), BF16),
            vmem((768, D), BF16),
            vmem((EXT, D), BF16),
            vmem((2 * GRID, D), BF16),
            vmem((2, GRID, D), BF16),
            vmem((2, 6, NODES, D), BF16),
            vmem((D, D), F32),
            vmem((2, 2, 4, 128, 256), BF16),
            vmem((2, 2, 3, 128, 256), BF16),
            vmem((2, 2, 4, 32, 256), BF16),
            vmem((2, 2, 3, 32, 256), BF16),
            vmem((2, 4, 16, 256), BF16),
            vmem((2, 7, 16, 256), BF16),
            vmem((2, 32, 256), BF16),
            vmem((8, 64, D), BF16),
            vmem((7, 64, D), BF16),
            vmem((4, 16, D), BF16),
            vmem((3, 16, D), BF16),
            vmem((2, 8, D), F32),
            vmem((4, 8, D), F32),
            vmem((2, 8, D), F32),
            dma((5,)),
            dma((2,)),
            dma((5,)),
            dma((2,)),
            dma((2,)),
            dma((9,)),
            dma((9,)),
            dma((12,)),
            dma,
            dma((18,)),
            dma((18,)),
            dma((21,)),
            dma((2,)),
            dma((18,)),
            dma((6,)),
            dma((9,)),
            dma((18,)),
            dma((18,)),
            dma((21,)),
            dma((3,)),
            dma((7,)),
            dma((7,)),
            dma((3,)),
            dma((3,)),
            dma((3,)),
            dma((4,)),
            dma,
            dma,
        ],
        compiler_params=pltpu.CompilerParams(
            collective_id=0, has_side_effects=True, vmem_limit_bytes=48 * 2**20
        ),
        name="edge_layer",
    )(
        *(
            array if array is enc_live else pltpu.with_memory_space_constraint(array, pltpu.HBM)
            for array in (
                grid_latent[0, 0],
                grid_cot[0, 0],
                mesh_latent[0, 0],
                mesh_cot[0, 0],
                processed[0, 0],
                enc_weights,
                dec_weights,
                enc_send[0, 0],
                enc_recv[0, 0],
                enc_live,
                dec_send.reshape(3, 1, 128),
                dec_recv.reshape(3, 1, 128),
            )
        )
    )
    return pl.pallas_call(
        write_out,
        out_shape=(
            jax.ShapeDtypeStruct((1, 1, GRID, D), BF16),
            jax.ShapeDtypeStruct((1, 1, NODES, D), BF16),
            jax.ShapeDtypeStruct((1, 1, NODES, D), BF16),
            jax.ShapeDtypeStruct((3, 8, D), F32),
            jax.ShapeDtypeStruct((3, 8, D), F32),
        ),
        in_specs=[pl.BlockSpec(memory_space=pltpu.VMEM)] * 4,
        out_specs=(pl.BlockSpec(memory_space=pltpu.HBM),) * 5,
        scratch_shapes=[dma((5,))],
        compiler_params=pltpu.CompilerParams(vmem_limit_bytes=2 * 2**20),
        name="write_out",
    )(*(pltpu.with_memory_space_constraint(array, pltpu.VMEM) for array in outs))


def solution(mesh):
    by_node = P("lat", "lon", None, None)
    return jax.shard_map(
        shards,
        mesh=mesh,
        in_specs=(by_node,) * 5 + (P(), P()) + (by_node, by_node, P("lat", "lon", None), by_node, by_node),
        out_specs=(by_node, by_node, by_node, P(None, "lon", None), P(None, "lon", None)),
        check_vma=False,
    )
```

```python
import math

import jax
import jax.numpy as jnp
from jax import lax
from jax.experimental import pallas as pl
from jax.experimental.pallas import tpu as pltpu
from jax.sharding import PartitionSpec as P

BF16 = jnp.bfloat16
F32 = jnp.float32
I32 = jnp.int32
MESH = pl.DeviceIdType.MESH
D = 512
GRID = 128
NODES = 64
SLOTS = 9
EXT = SLOTS * NODES


def dot(a, b):
    return lax.dot_general(a, b, (((1,), (0,)), ((), ())), preferred_element_type=F32)


def dot_bt(a, b):
    return lax.dot_general(a, b, (((1,), (1,)), ((), ())), preferred_element_type=F32)


def dot_at(a, b):
    return lax.dot_general(a, b, (((0,), (0,)), ((), ())), preferred_element_type=F32)


def pick_rows(index_row, rows):
    return jnp.where(lax.broadcasted_iota(I32, (rows, 128), 0) == index_row, 1.0, 0.0).astype(BF16)


def pick_cols(index_row, columns):
    turned = jnp.transpose(jnp.broadcast_to(index_row, (128, 128)))
    lane = lax.broadcasted_iota(I32, (128, 128), 1)
    parts = []
    for start in range(0, columns, 128):
        part = jnp.where(turned == lane + start, 1.0, 0.0).astype(BF16)
        parts.append(part[:, : min(128, columns - start)])
    return parts[0] if len(parts) == 1 else jnp.concatenate(parts, 1)


def kernel(
    grid_ref,
    cot_ref,
    mesh_ref,
    mcot_ref,
    proc_ref,
    encw_ref,
    decw_ref,
    esend_ref,
    erecv_ref,
    live_ref,
    dsend_ref,
    drecv_ref,
    grid_out,
    mesh_out,
    proc_out,
    weights_out,
    wts,
    gall,
    call,
    mext,
    text,
    town,
    ebuf,
    dbuf,
    lbuf,
    lone,
    mpick,
    mturn,
    gturn,
    gproj,
    mproj,
    gpart,
    back,
    hid,
    msg,
    pgrad,
    part,
    gsum,
    gboth,
    fold,
    dwbuf,
    send1,
    recv1,
    send2,
    recv2,
    send3,
    recv3,
    final,
    zsend,
    zrecv,
    xsend,
    xrecv,
    ysend,
    yrecv,
    last,
    w_sem,
    own_sem,
    i_sem,
    g_sem,
    c_sem,
    m_sem,
    t_sem,
    f_sem,
    gs_sem,
    r1_sem,
    r2_sem,
    r3_sem,
    r4_sem,
    hs_sem,
    ss_sem,
    fs_sem,
    s1_sem,
    s2_sem,
    s3_sem,
    s4_sem,
    zs_sem,
    zr_sem,
    xs_sem,
    xr_sem,
    ys_sem,
    yr_sem,
    ls_sem,
    lr_sem,
    grad_scale,
):
    lat = lax.axis_index("lat")
    lon = lax.axis_index("lon")
    yh = lax.div(lat, 2)
    core = lax.rem(lat, 2)
    z = lax.div(lon, 8)
    yl = lax.rem(lax.div(lon, 4), 2)
    x = lax.rem(lon, 4)
    y = yh * 2 + yl
    sib = (yh * 2 + (1 - core), lon)
    adjacent = core == 1 - yh

    def lon_of(zz, yy, xx):
        return zz * 8 + yy * 4 + xx

    def sector(step):
        return lax.rem(lon + step + 64, 64)

    def x_dev(xx):
        return (lat, lon_of(z, yl, xx))

    def y_dev(yy):
        return (lax.div(yy, 2) * 2 + core, lon_of(z, lax.rem(yy, 2), x))

    def z_dev(zz):
        return (lat, lon_of(zz, yl, x))

    def rcopy(src, dst, ssem, rsem, dev):
        return pltpu.make_async_remote_copy(
            src_ref=src, dst_ref=dst, send_sem=ssem, recv_sem=rsem, device_id=dev, device_id_type=MESH
        )

    def arrived(dst, rsem):
        pltpu.make_async_copy(dst, dst, rsem).wait()

    def load(src, dst, sem):
        pltpu.make_async_copy(src, dst, sem).start()

    load(encw_ref.at[0], wts.at[0], w_sem.at[0])
    load(decw_ref.at[1], wts.at[3], w_sem.at[3])
    load(encw_ref.at[1], wts.at[1], w_sem.at[1])
    load(decw_ref.at[0], wts.at[2], w_sem.at[2])

    @pl.when(core == 0)
    def _():
        load(encw_ref.at[2], wts.at[4], w_sem.at[4])
        load(esend_ref, ebuf.at[0, 0], i_sem.at[0])
        load(erecv_ref, ebuf.at[0, 1], i_sem.at[1])
        load(mesh_ref, mext.at[pl.ds(pl.multiple_of((yh * 3 + 1) * NODES, NODES), NODES)], m_sem.at[yh * 3 + 1])
        load(mcot_ref, text.at[pl.ds(pl.multiple_of((yh * 3 + 1) * NODES, NODES), NODES)], t_sem.at[yh * 3 + 1])

    @pl.when(core == 1)
    def _():
        load(decw_ref.at[2], wts.at[4], w_sem.at[4])
        load(dsend_ref, dbuf.at[1, 0], i_sem.at[2])
        load(drecv_ref, dbuf.at[1, 1], i_sem.at[3])
        slot = (yh + 1) * 3 + 1
        load(proc_ref, mext.at[pl.ds(pl.multiple_of(slot * NODES, NODES), NODES)], m_sem.at[slot])

    own_rows = pl.ds(pl.multiple_of(core * GRID, GRID), GRID)
    load(grid_ref, gall.at[own_rows], g_sem.at[core])
    load(cot_ref, call.at[own_rows], c_sem.at[core])
    load(mcot_ref, town, own_sem.at[0])
    load(live_ref, lone, own_sem.at[1])

    barrier = pltpu.get_barrier_semaphore()
    greeted = []
    for dyh in (0, 1):
        for dc in (0, 1):
            for step in (-1, 0, 1):
                if (dyh, dc, step) != (0, 0, 0):
                    to_yh = yh if dyh == 0 else 1 - yh
                    to_core = core if dc == 0 else 1 - core
                    greeted.append((to_yh * 2 + to_core, sector(step)))
    for step in range(1, 4):
        greeted.append(x_dev(lax.rem(x + step, 4)))
        greeted.append(y_dev(lax.rem(y + step, 4)))
    for step in range(1, 8):
        greeted.append(z_dev(lax.rem(z + step, 8)))
    for dev in greeted:
        pl.semaphore_signal(barrier, inc=1, device_id=dev, device_id_type=MESH)
    pl.semaphore_wait(barrier, len(greeted))

    def halo_copy(which, side, step):
        to_yh = yh if side == 0 else 1 - yh
        slot = (lat - to_yh) * 3 + 1 - step
        rows = pl.ds(pl.multiple_of(slot * NODES, NODES), NODES)
        at = side * 9 + (step + 1) * 3
        enc_dev = (to_yh * 2, sector(step))
        dec_dev = (to_yh * 2 + 1, sector(step))
        if which == 0:
            return rcopy(mesh_ref, mext.at[rows], hs_sem.at[at], m_sem.at[slot], enc_dev)
        if which == 1:
            return rcopy(mcot_ref, text.at[rows], hs_sem.at[at + 1], t_sem.at[slot], enc_dev)
        return rcopy(proc_ref, mext.at[rows], hs_sem.at[at + 2], m_sem.at[slot], dec_dev)

    def each_halo(which, action):
        @pl.when(adjacent)
        def _():
            for step in (1, -1, 0):
                action(halo_copy(which, 1, step))

        for step in (1, -1):
            action(halo_copy(which, 0, step))

        @pl.when(core == (0 if which == 2 else 1))
        def _():
            action(halo_copy(which, 0, 0))

    cross_band = 2 - 2 * yh

    def each_swap(action):
        action(rcopy(grid_ref, gall.at[own_rows], ss_sem.at[0], g_sem.at[core], sib))

        @pl.when(core == 0)
        def _():
            action(rcopy(dsend_ref, dbuf.at[0, 0], ss_sem.at[1], i_sem.at[0], sib))
            action(rcopy(drecv_ref, dbuf.at[0, 1], ss_sem.at[4], i_sem.at[1], sib))
            action(rcopy(cot_ref, call.at[pl.ds(0, GRID)], ss_sem.at[2], c_sem.at[0], sib))

        @pl.when(core == 1)
        def _():
            action(rcopy(esend_ref, ebuf.at[1, 0], ss_sem.at[1], i_sem.at[2], sib))
            action(rcopy(erecv_ref, ebuf.at[1, 1], ss_sem.at[4], i_sem.at[3], sib))
            action(rcopy(lbuf.at[1], lbuf.at[1], ss_sem.at[5], i_sem.at[4], sib))

    each_halo(2, lambda copy: copy.start())
    each_halo(0, lambda copy: copy.start())
    arrived(lone, own_sem.at[1])
    lbuf[core] = jnp.broadcast_to(lone[0], (8, 128))
    each_swap(lambda copy: copy.start())
    each_halo(1, lambda copy: copy.start())

    @pl.when(jnp.logical_not(adjacent))
    def _():
        for role in (0, 1):
            for k in (3, 4, 5):
                fold[role, k] = jnp.zeros((NODES, D), BF16)

    def by_core(of_core0, of_core1):
        if isinstance(of_core0, tuple):
            return tuple(jnp.where(core == 0, a, b) for a, b in zip(of_core0, of_core1))
        return jnp.where(core == 0, of_core0, of_core1)

    def toward_x(step):
        to = lax.rem(x + step, 4)
        return to, x_dev(to)

    def toward_y(step):
        to = lax.rem(y + step, 4)
        return to, y_dev(to)

    def toward(mat, half, stage, step):
        if mat == 2:
            of_x, of_y = toward_x(step), toward_y(step)
            first, second = (of_y, of_x) if stage == 1 else (of_x, of_y)
            return by_core(first[0], second[0]), by_core(first[1], second[1])
        return toward_x(step) if half + 1 == stage else toward_y(step)

    units = ((0, 0), (0, 1), (1, 0), (1, 1), (2, 0))

    def stage1_copies(mat, half):
        copies = []
        for step in (1, 3, 2):
            to, dev = toward(mat, half, 1, step)
            sem = (mat * 2 + half) * 3 + step - 1
            copies.append(
                rcopy(send1.at[mat, half, to], recv1.at[mat, half, step - 1], s1_sem.at[sem], r1_sem.at[sem], dev)
            )
        return copies

    def stage2_copies(mat, half):
        copies = []
        for step in (1, 3, 2):
            to, dev = toward(mat, half, 2, step)
            sem = (mat * 2 + half) * 3 + step - 1
            copies.append(
                rcopy(send2.at[mat, half, to], recv2.at[mat, half, step - 1], s2_sem.at[sem], r2_sem.at[sem], dev)
            )
        return copies

    def row_group(xx, yy, zz):
        return ((yy // 2) * 4 + zz) * 64 + (yy % 2) * 32 + xx * 8

    def send_matrix(mat):
        for xx in range(4):
            pieces = []
            for yy in range(4):
                for zz in range(4):
                    row = row_group(xx, yy, zz)
                    pieces.append(dwbuf[row : row + 8, 0:256])
            send1[mat, 0, xx] = jnp.concatenate(pieces, 0).astype(BF16)
        for yy in range(4):
            pieces = []
            for xx in range(4):
                for zz in range(4):
                    row = row_group(xx, yy, zz)
                    pieces.append(dwbuf[row : row + 8, 256:512])
            send1[mat, 1, yy] = jnp.concatenate(pieces, 0).astype(BF16)
        for half in (0, 1):
            for copy in stage1_copies(mat, half):
                copy.start()

    def z_copies():
        copies = []
        for step in (4, 3, 5, 2, 6, 1, 7):
            to = lax.rem(z + step, 8)
            copies.append(rcopy(zsend.at[to], zrecv.at[step - 1], zs_sem.at[step - 1], zr_sem.at[step - 1], z_dev(to)))
        return copies

    def x_copies():
        copies = []
        for step in (2, 1, 3):
            to = lax.rem(x + step, 4)
            copies.append(rcopy(xsend.at[to], xrecv.at[step - 1], xs_sem.at[step - 1], xr_sem.at[step - 1], x_dev(to)))
        return copies

    def y_copies():
        copies = []
        for step in (2, 1, 3):
            to = lax.rem(y + step, 4)
            copies.append(rcopy(ysend.at[lax.rem(to, 2)], yrecv.at[y], ys_sem.at[step - 1], yr_sem.at[y], y_dev(to)))
        return copies

    def sibling_copy():
        return rcopy(last.at[core], last.at[core], ls_sem, lr_sem, sib)

    def send_out_matrix(role):
        for zz in range(8):
            zsend[zz] = dwbuf[zz * 64 : (zz + 1) * 64, 0:256].astype(BF16)
        for copy in z_copies():
            copy.start()
        for to in range(4):
            pieces = []
            for other in range(4):
                for zz in range(4):
                    row = row_group(other, to, zz) if role == 0 else row_group(to, other, zz)
                    pieces.append(dwbuf[row : row + 8, 256:512])
            send1[2, 0, to] = jnp.concatenate(pieces, 0).astype(BF16)
        for copy in stage1_copies(2, 0):
            copy.start()

    def fold_copies(side, step):
        copies = []
        for which in ((0, 1) if side == 0 else (2,)):
            slot = ((yh + which) if side == 0 else cross_band) * 3 + 1 + step
            dev = (yh * 2 + which if side == 0 else (1 - yh) * 2 + yh, sector(step))
            rows = pl.ds(pl.multiple_of(slot * NODES, NODES), NODES)
            k = side * 3 + 1 - step
            copies.append(
                rcopy(part.at[rows], fold.at[core, k], fs_sem.at[which * 3 + step + 1], f_sem.at[core * 6 + k], dev)
            )
        return copies

    def each_fold(role, action):
        for step in (1, -1, 0):
            action(fold_copies(1, step)[0])
        for step in (1, -1):
            for copy in fold_copies(0, step):
                action(copy)
        action(fold_copies(0, 0)[1 - role])

    def gsum_copy():
        other = pl.ds(pl.multiple_of((1 - core) * GRID, GRID), GRID)
        return rcopy(gsum.at[other], gboth.at[core], ss_sem.at[3], gs_sem, sib)

    def weight(k):
        pltpu.make_async_copy(wts.at[k], wts.at[k], w_sem.at[k]).wait()

    def wait_band(band):
        for col in range(3):
            slot = band * 3 + col
            rows = pl.ds(pl.multiple_of(slot * NODES, NODES), NODES)
            arrived(mext.at[rows], m_sem.at[slot])

    def wait_cot(band):
        for col in range(3):
            slot = band * 3 + col
            rows = pl.ds(pl.multiple_of(slot * NODES, NODES), NODES)
            arrived(text.at[rows], t_sem.at[slot])

    def network(role):
        blocks = 2 if role == 0 else 3
        edges = blocks * 128
        w_grid, w_mesh = (0, 1) if role == 0 else (3, 2)
        for band in (0, 1):
            arrived(gall.at[pl.ds(band * GRID, GRID)], g_sem.at[band])
        weight(w_grid)
        gproj[...] = dot(gall[...], wts[w_grid]).astype(BF16)
        picks = ebuf if role == 0 else dbuf
        for band in (0, 1):
            for which in (0, 1):
                arrived(picks.at[band, which], i_sem.at[band * 2 + which])
        if role == 0:
            arrived(lbuf.at[1], i_sem.at[4])

        def rows_of(band, which):
            if role == 0:
                both = picks[band, which]
                return [both[q : q + 1] for q in range(blocks)]
            return [picks[band, which, q] for q in range(blocks)]

        grid_rows = [rows_of(b, role) for b in (0, 1)]
        mesh_rows = [[r + 192 * (yh + b - 1) for r in rows_of(b, 1 - role)] for b in (0, 1)]
        weight(4)
        for b in (0, 1):
            rows = slice(b * edges, (b + 1) * edges)
            g_pick = jnp.concatenate([pick_cols(r, GRID) for r in grid_rows[b]], 0)
            gpart[rows] = dot(g_pick, gproj[b * GRID : (b + 1) * GRID])
            if role == 1:
                arrived(call.at[pl.ds(b * GRID, GRID)], c_sem.at[b])
                picked = dot(g_pick, call[b * GRID : (b + 1) * GRID]).astype(BF16)
                msg[rows] = picked
                back[rows] = dot_bt(picked, wts[4])
        for b in (0, 1):
            for q in range(blocks):
                at = b * edges + q * 128
                mpick[at : at + 128] = pick_cols(mesh_rows[b][q], EXT)
                mturn[:, at : at + 128] = pick_rows(mesh_rows[b][q], EXT)
                gturn[:, at : at + 128] = pick_rows(grid_rows[b][q], GRID)
        weight(w_mesh)
        for k in (0, 1, 2):
            band = (yh + k if k < 2 else cross_band)
            wait_band(band)
            rows = pl.ds(pl.multiple_of(band * 192, 192), 192)
            mproj[rows] = dot(mext[rows], wts[w_mesh]).astype(BF16)
        for b in (0, 1):
            rows = slice(b * edges, (b + 1) * edges)
            pre = dot(mpick[rows], mproj[...]) + gpart[rows]
            gate = 1.0 / (1.0 + jnp.exp(-pre))
            hid[rows] = (pre * gate).astype(BF16)
            gpart[rows] = gate * (1.0 + pre * (1.0 - gate))
        if role == 0:
            for band in range(3):
                wait_cot(band)
            for b in (0, 1):
                rows = slice(b * edges, (b + 1) * edges)
                place = lax.broadcasted_iota(I32, (edges, D), 0)
                live = lbuf[b, 0:1, 0:1]
                picked = jnp.where(place < live, dot(mpick[rows], text[...]), 0.0).astype(BF16)
                msg[rows] = picked
        every = slice(0, 2 * edges)
        dwbuf[...] = dot_at(hid[every], msg[every])
        send_out_matrix(role)
        if role == 0:
            back[every] = dot_bt(msg[every], wts[4])
        pgrad[every] = (back[every] * gpart[every]).astype(BF16)
        part[...] = dot(mturn[:, every], pgrad[every]).astype(BF16)
        if role == 1:
            each_fold(1, lambda copy: copy.start())
            dwbuf[...] = dot_at(mext[...], part[...])
            send_matrix(0)
        for b in (0, 1):
            rows = slice(b * edges, (b + 1) * edges)
            gsum[b * GRID : (b + 1) * GRID] = dot(gturn[:, rows], pgrad[rows]).astype(BF16)
        gsum_copy().start()
        dwbuf[...] = dot_at(gall[...], gsum[...])
        send_matrix(0 if role == 0 else 1)
        if role == 0:
            dwbuf[...] = dot_at(mext[...], part[...])
            send_matrix(1)

    @pl.when(core == 0)
    def _():
        network(0)

    @pl.when(core == 1)
    def _():
        network(1)

    @pl.when(core == 0)
    def _():
        for k in (2, 3):
            weight(k)
        arrived(call.at[own_rows], c_sem.at[0])

    @pl.when(core == 1)
    def _():
        for k in (0, 1):
            weight(k)

    arrived(town, own_sem.at[0])

    for mat, half in ((2, 0), (0, 0), (0, 1), (1, 0), (1, 1)):
        for step in range(3):
            sem = (mat * 2 + half) * 3 + step
            arrived(recv1.at[mat, half, step], r1_sem.at[sem])
        own = by_core(y, x) if mat == 2 else (x, y)[half]
        total = send1[mat, half, own].astype(F32)
        for step in range(3):
            total = total + recv1[mat, half, step].astype(F32)
        total = total.astype(BF16)
        for k in range(4):
            send2[mat, half, k] = total[k * 32 : (k + 1) * 32]
        for copy in stage2_copies(mat, half):
            copy.start()

    total = zsend[z].astype(F32)
    for step in range(1, 8):
        arrived(zrecv.at[step - 1], zr_sem.at[step - 1])
        total = total + zrecv[step - 1].astype(F32)
    for xx in range(4):
        xsend[xx] = jnp.concatenate([total[xx * 8 : xx * 8 + 8], total[32 + xx * 8 : 40 + xx * 8]], 0).astype(BF16)
    for copy in x_copies():
        copy.start()

    holds = lax.div(z, 4) == yh

    def each_stage3(mat, action):
        for step in (4, 3, 5, 2, 6, 1, 7):
            to = lax.rem(z + step, 8)

            @pl.when(lax.div(to, 4) == yh)
            def _():
                sem = mat * 7 + step - 1
                action(
                    rcopy(send3.at[mat, lax.rem(to, 4)], recv3.at[mat, step - 1], s3_sem.at[sem], r3_sem.at[sem], z_dev(to))
                )

    def stage3(mat):
        sums = []
        for half in (0, 1) if mat < 2 else (0,):
            for step in range(3):
                sem = (mat * 2 + half) * 3 + step
                arrived(recv2.at[mat, half, step], r2_sem.at[sem])
            own = by_core(x, y) if mat == 2 else (y, x)[half]
            total = send2[mat, half, own].astype(F32)
            for step in range(3):
                total = total + recv2[mat, half, step].astype(F32)
            sums.append(total)
        for q in range(4):
            pieces = [t[q * 8 : (q + 1) * 8] for t in sums]
            if mat == 2:
                pieces.append(jnp.zeros((8, 256), F32))
            send3[mat, q] = jnp.concatenate(pieces, 0).astype(BF16)
        each_stage3(mat, lambda copy: copy.start())

    stage3(2)
    stage3(0)

    @pl.when(core == 0)
    def _():
        each_fold(0, lambda copy: copy.start())

    stage3(1)

    total = xsend[x].astype(F32)
    for step in range(1, 4):
        arrived(xrecv.at[step - 1], xr_sem.at[step - 1])
        total = total + xrecv[step - 1].astype(F32)
    ysend[0] = total[0:8]
    ysend[1] = total[8:16]
    for copy in y_copies():
        copy.start()

    gboth[core] = gsum[own_rows]
    arrived(gboth.at[1 - core], gs_sem)
    grid_out[...] = (call[own_rows].astype(F32) + dot_bt(gboth[0], wts[0]) + dot_bt(gboth[1], wts[3])).astype(BF16)

    each_swap(lambda copy: copy.wait_send())
    for which in range(3):
        each_halo(which, lambda copy: copy.wait_send())
    gsum_copy().wait_send()
    for copy in z_copies() + x_copies():
        copy.wait_send()
    for mat, half in units:
        for copy in stage1_copies(mat, half) + stage2_copies(mat, half):
            copy.wait_send()

    def last_copies():
        devs = (((1 - yh) * 2 + core, lon), ((1 - yh) * 2 + 1 - core, lon), sib)
        return [rcopy(final.at[core], final.at[core], s4_sem.at[k], r4_sem.at[core], dev) for k, dev in enumerate(devs)]

    @pl.when(holds)
    def _():
        totals = []
        for mat in (2, 0, 1):
            for step in range(1, 8):
                arrived(recv3.at[mat, step - 1], r3_sem.at[mat * 7 + step - 1])
        for mat in range(3):
            total = send3[mat, lax.rem(z, 4)].astype(F32)
            for step in range(1, 8):
                total = total + recv3[mat, step - 1].astype(F32)
            totals.append(total)
        total = jnp.concatenate(totals, 0)
        final[core] = (total * grad_scale).astype(BF16)
        for copy in last_copies():
            copy.start()

    yrecv[y] = ysend[yl]
    for step in (1, 3, 2):
        beyond = lax.rem(y + step, 4)
        arrived(yrecv.at[beyond], yr_sem.at[beyond])
    last[core] = (yrecv[0] + yrecv[1] + yrecv[2] + yrecv[3]) * grad_scale
    sibling_copy().start()

    def part_of(slot):
        return pl.ds(pl.multiple_of(slot * NODES, NODES), NODES)

    def fold_wait(role, k):
        arrived(fold.at[role, k], f_sem.at[role * 6 + k])

    for role in (0, 1):
        for k in (0, 2):
            fold_wait(role, k)
    own_slot = part_of((yh + core) * 3 + 1)

    @pl.when(core == 0)
    def _():
        fold_wait(1, 1)
        fold[0, 1] = part[own_slot]

    @pl.when(core == 1)
    def _():
        fold_wait(0, 1)
        fold[1, 1] = part[own_slot]

    @pl.when(adjacent)
    def _():
        for role in (0, 1):
            for k in (3, 4, 5):
                fold_wait(role, k)

    def folded(role):
        total = fold[role, 0].astype(F32)
        for k in range(1, 6):
            total = total + fold[role, k].astype(F32)
        return total.astype(BF16)

    mesh_out[...] = (town[...].astype(F32) + dot_bt(folded(0), wts[1])).astype(BF16)
    proc_out[...] = dot_bt(folded(1), wts[2]).astype(BF16)

    @pl.when(holds)
    def _():
        arrived(final.at[1 - core], r4_sem.at[1 - core])

    @pl.when(jnp.logical_not(holds))
    def _():
        arrived(final.at[0], r4_sem.at[0])
        arrived(final.at[1], r4_sem.at[1])

    arrived(last.at[1 - core], lr_sem)
    for role in (0, 1):
        pieces = final[role].astype(F32)
        weights_out[role, 2, :, 0:256] = last[role]
        weights_out[role, 2, :, 256:512] = pieces[32:40]
        for mat in (0, 1):
            weights_out[role, mat, :, 0:256] = pieces[mat * 16 : mat * 16 + 8]
            weights_out[role, mat, :, 256:512] = pieces[mat * 16 + 8 : mat * 16 + 16]

    @pl.when(core == 0)
    def _():
        each_fold(0, lambda copy: copy.wait_send())

    @pl.when(core == 1)
    def _():
        each_fold(1, lambda copy: copy.wait_send())


    for copy in y_copies() + [sibling_copy()]:
        copy.wait_send()
    for mat in range(3):
        each_stage3(mat, lambda copy: copy.wait_send())

    @pl.when(holds)
    def _():
        for copy in last_copies():
            copy.wait_send()


def write_out(grid_in, mesh_in, proc_in, weights_in, grid_out, mesh_out, proc_out, enc_out, dec_out, sem):
    copies = [
        pltpu.make_async_copy(grid_in, grid_out.at[0, 0], sem.at[0]),
        pltpu.make_async_copy(mesh_in, mesh_out.at[0, 0], sem.at[1]),
        pltpu.make_async_copy(proc_in, proc_out.at[0, 0], sem.at[2]),
        pltpu.make_async_copy(weights_in.at[0], enc_out, sem.at[3]),
        pltpu.make_async_copy(weights_in.at[1], dec_out, sem.at[4]),
    ]
    for copy in copies:
        copy.start()
    for copy in copies:
        copy.wait()


def shards(
    grid_latent,
    grid_cot,
    mesh_latent,
    mesh_cot,
    processed,
    enc_weights,
    dec_weights,
    enc_send,
    enc_recv,
    enc_live,
    dec_send,
    dec_recv,
):
    grad_scale = 1.0 / math.sqrt(4 * 64 * 128)
    vmem = pltpu.VMEM
    dma = pltpu.SemaphoreType.DMA
    outs = pl.pallas_call(
        lambda *refs: kernel(*refs, grad_scale),
        out_shape=(
            jax.ShapeDtypeStruct((GRID, D), BF16),
            jax.ShapeDtypeStruct((NODES, D), BF16),
            jax.ShapeDtypeStruct((NODES, D), BF16),
            jax.ShapeDtypeStruct((2, 3, 8, D), F32),
        ),
        in_specs=[pl.BlockSpec(memory_space=pltpu.HBM)] * 12,
        out_specs=(pl.BlockSpec(memory_space=pltpu.VMEM),) * 4,
        scratch_shapes=[
            vmem((5, D, D), BF16),
            vmem((2 * GRID, D), BF16),
            vmem((2 * GRID, D), BF16),
            vmem((EXT, D), BF16),
            vmem((EXT, D), BF16),
            vmem((NODES, D), BF16),
            vmem((2, 2, 2, 128), I32),
            vmem((2, 2, 3, 1, 128), I32),
            vmem((2, 8, 128), I32),
            vmem((1, 1, 1), I32),
            vmem((768, EXT), BF16),
            vmem((EXT, 768), BF16),
            vmem((GRID, 768), BF16),
            vmem((2 * GRID, D), BF16),
            vmem((EXT, D), BF16),
            vmem((768, D), F32),
            vmem((768, D), F32),
            vmem((768, D), BF16),
            vmem((768, D), BF16),
            vmem((768, D), BF16),
            vmem((EXT, D), BF16),
            vmem((2 * GRID, D), BF16),
            vmem((2, GRID, D), BF16),
            vmem((2, 6, NODES, D), BF16),
            vmem((D, D), F32),
            vmem((3, 2, 4, 128, 256), BF16),
            vmem((3, 2, 3, 128, 256), BF16),
            vmem((3, 2, 4, 32, 256), BF16),
            vmem((3, 2, 3, 32, 256), BF16),
            vmem((3, 4, 16, 256), BF16),
            vmem((3, 7, 16, 256), BF16),
            vmem((2, 48, 256), BF16),
            vmem((8, 64, 256), BF16),
            vmem((7, 64, 256), BF16),
            vmem((4, 16, 256), BF16),
            vmem((3, 16, 256), BF16),
            vmem((2, 8, 256), F32),
            vmem((4, 8, 256), F32),
            vmem((2, 8, 256), F32),
            dma((5,)),
            dma((2,)),
            dma((5,)),
            dma((2,)),
            dma((2,)),
            dma((9,)),
            dma((9,)),
            dma((12,)),
            dma,
            dma((18,)),
            dma((18,)),
            dma((21,)),
            dma((2,)),
            dma((18,)),
            dma((6,)),
            dma((9,)),
            dma((18,)),
            dma((18,)),
            dma((21,)),
            dma((3,)),
            dma((7,)),
            dma((7,)),
            dma((3,)),
            dma((3,)),
            dma((3,)),
            dma((4,)),
            dma,
            dma,
        ],
        compiler_params=pltpu.CompilerParams(
            collective_id=0, has_side_effects=True, vmem_limit_bytes=48 * 2**20
        ),
        name="edge_layer",
    )(
        *(
            array if array is enc_live else pltpu.with_memory_space_constraint(array, pltpu.HBM)
            for array in (
                grid_latent[0, 0],
                grid_cot[0, 0],
                mesh_latent[0, 0],
                mesh_cot[0, 0],
                processed[0, 0],
                enc_weights,
                dec_weights,
                enc_send[0, 0],
                enc_recv[0, 0],
                enc_live,
                dec_send.reshape(3, 1, 128),
                dec_recv.reshape(3, 1, 128),
            )
        )
    )
    return pl.pallas_call(
        write_out,
        out_shape=(
            jax.ShapeDtypeStruct((1, 1, GRID, D), BF16),
            jax.ShapeDtypeStruct((1, 1, NODES, D), BF16),
            jax.ShapeDtypeStruct((1, 1, NODES, D), BF16),
            jax.ShapeDtypeStruct((3, 8, D), F32),
            jax.ShapeDtypeStruct((3, 8, D), F32),
        ),
        in_specs=[pl.BlockSpec(memory_space=pltpu.VMEM)] * 4,
        out_specs=(pl.BlockSpec(memory_space=pltpu.HBM),) * 5,
        scratch_shapes=[dma((5,))],
        compiler_params=pltpu.CompilerParams(vmem_limit_bytes=2 * 2**20),
        name="write_out",
    )(*(pltpu.with_memory_space_constraint(array, pltpu.VMEM) for array in outs))


def solution(mesh):
    by_node = P("lat", "lon", None, None)
    return jax.shard_map(
        shards,
        mesh=mesh,
        in_specs=(by_node,) * 5 + (P(), P()) + (by_node, by_node, P("lat", "lon", None), by_node, by_node),
        out_specs=(by_node, by_node, by_node, P(None, "lon", None), P(None, "lon", None)),
        check_vma=False,
    )
```
